32 devices in a mesh: row: 8 (over y, x, core), col: 4 (over z).
Axes of the slice: x: 2, y: 2, z: 4, core: 2. Of those that a mesh axis runs over, the one named last changes fastest.
Arguments:
- front_inverse: bfloat16 [24576, 24576], P('row', 'col'), may hold values from -0.0390625 to 0.0390625
- coupling_tiles: bfloat16 [768, 128, 128], P('col'), may hold values from -12 to 12
- tile_row: int32 [768], P('col'), may hold values from 0 to 191, as said below
- tile_col: int32 [768], P('col'), may hold values from 0 to 15
- surface_map: int32 [2, 8192], P(None, 'row'), may hold values from 0 to 24575, as said below
- bem_entries: bfloat16 [2, 8192, 2048], P(None, 'row', 'col'), may hold values from -6 to 6
- pivot_inverse: bfloat16 [8192, 8192], P('row'), may hold values from -0.0625 to 0.0625
- slab_below: bfloat16 [8192, 8192], P('row'), may hold values from -0.0625 to 0.0625
Outputs:
- panel_out: bfloat16 [2, 8192, 2048], P(None, 'row', 'col')
The draws below stay inside these ranges and needn't reach their ends.
Inputs may be any that keep to these rules, and one draw needn't show every extreme that they name: `tile_row`: tiles at positions c * 192 to (c + 1) * 192 - 1 lie in block rows c * 48 to (c + 1) * 48 - 1; no two tiles share both block row and block column. `surface_map`: all entries differ; of the entries in the columns of one index of row, at most 384 lie in any one block of 3072 front rows that starts at a multiple of 3072, and for every index of row some block holds exactly 384 of them.
All inputs are finite; a program needn't handle non-finite values.
Results may differ from the reference program's by a relative error of at most 0.0058.
Values may be sent and summed in bfloat16 or wider, within the bound.
No kernel may reach another device: no remote copies, remote signals or barrier semaphores. Data moves between devices by JAX's collectives and lax.ppermute only.
A program may use at most 384 MiB of HBM per device.

```python
import jax
import jax.numpy as jnp

NF = 24576
KS = 8192
COLS = 2048
BR_COL = 48
TILES_COL = 192
ROUTE_CAP = 384
N_ROW = 8
N_COL = 4


def tile_pairs(key):
    base_key = jax.random.fold_in(key, 7)
    col_blocks = COLS // 128
    slot_total = BR_COL * col_blocks
    shards = NF // (128 * BR_COL)

    def shard_draw(shard):
        picked = jax.random.permutation(jax.random.fold_in(base_key, shard), slot_total)[:TILES_COL]
        return (shard * BR_COL + picked // col_blocks, picked % col_blocks)
    block_rows, block_cols = jax.vmap(shard_draw)(jnp.arange(shards, dtype=jnp.int32))
    return (block_rows.reshape(-1).astype(jnp.int32), block_cols.reshape(-1).astype(jnp.int32))


def draw_tile_row(key, part):
    return tile_pairs(key)[0]


def draw_tile_col(key, part):
    return tile_pairs(key)[1]


def draw_surface_map(key, part):
    base_key = jax.random.fold_in(key, 11)
    row_width = NF // N_ROW
    per_device = 2 * (KS // N_ROW)
    capacity = ROUTE_CAP
    shuffle_key = jax.random.fold_in(base_key, 1)
    shuffles = jax.vmap(lambda owner: jax.random.permutation(jax.random.fold_in(shuffle_key, owner), row_width))(jnp.arange(N_ROW, dtype=jnp.int32))

    def device_draw(device):
        device_key = jax.random.fold_in(jax.random.fold_in(base_key, 2), device)
        owner_order = jax.random.permutation(jax.random.fold_in(device_key, 0), N_ROW)
        entry = jnp.arange(per_device, dtype=jnp.int32)
        later = jnp.maximum(entry - capacity, 0)
        spot = jnp.where(entry < capacity, 0, 1 + later % (N_ROW - 1))
        within = jnp.where(entry < capacity, entry, later // (N_ROW - 1))
        owners = owner_order[spot]
        front_rows = owners * row_width + shuffles[owners, device * capacity + within]
        order = jax.random.permutation(jax.random.fold_in(device_key, 1), per_device)
        return front_rows[order]
    every = jax.vmap(device_draw)(jnp.arange(N_ROW, dtype=jnp.int32))
    every = every.reshape(N_ROW, 2, KS // N_ROW).transpose(1, 0, 2).reshape(2, KS)
    return every.astype(jnp.int32)


def block_scale(rng, dims, cuts, least, high):
    level, own = 1.0, jax.random.fold_in(rng, 6)
    for dim, parts in cuts:
        heights = jnp.exp(jax.random.uniform(jax.random.fold_in(own, dim), (parts,), jnp.float32, least / len(cuts), high / len(cuts)))
        level = level * jnp.repeat(heights, dims[dim] // parts).reshape([-1 if axis == dim else 1 for axis in range(len(dims))])
    return level


def normal_values(stream_key, dims, spread, reach, pieces=(), kind=jnp.bfloat16):
    drawn = jax.random.normal(stream_key, dims, jnp.float32) * spread
    if len(pieces) > 0:
        drawn = block_scale(stream_key, dims, pieces, -0.22, 0.18) * drawn
    return jnp.clip(drawn, min=-reach, max=reach).astype(kind)


def setup_inputs(seed: int = 0) -> dict:
    key_of = jax.random.split(jax.random.key(seed), 9)
    return {
        "front_inverse": normal_values(key_of[0], (NF, NF), NF ** -0.5, 0.0390625, ((0, 8), (1, 4))),
        "coupling_tiles": normal_values(key_of[1], (N_COL * TILES_COL, 128, 128), 2.0, 12.0, ((0, 4),)),
        "tile_row": draw_tile_row(jax.random.fold_in(key_of[8], 71), 0),
        "tile_col": draw_tile_col(jax.random.fold_in(key_of[8], 71), 0),
        "surface_map": draw_surface_map(jax.random.fold_in(key_of[8], 71), 0),
        "bem_entries": normal_values(key_of[5], (2, KS, COLS), 1.0, 6.0, ((1, 8), (2, 4))),
        "pivot_inverse": normal_values(key_of[6], (KS, KS), KS ** -0.5, 0.0625, ((0, 8),)),
        "slab_below": normal_values(key_of[7], (KS, KS), KS ** -0.5, 0.0625, ((0, 8),)),
    }


def reference(front_inverse, coupling_tiles, tile_row, tile_col, surface_map, bem_entries, pivot_inverse, slab_below):
    col_blocks = COLS // 128
    blocks = jnp.zeros((NF // 128, col_blocks, 128, 128), jnp.bfloat16)
    blocks = blocks.at[tile_row, tile_col].set(coupling_tiles)
    coupling = blocks.transpose(0, 2, 1, 3).reshape(NF, COLS)
    selected = front_inverse[surface_map.reshape(-1)]
    schur_part = jnp.dot(selected, coupling, preferred_element_type=jnp.float32).astype(jnp.bfloat16)
    schur_part = schur_part.reshape(2, KS, COLS)
    assembled = (bem_entries.astype(jnp.float32) - schur_part.astype(jnp.float32)).astype(jnp.bfloat16)
    pivot_solved = jnp.dot(pivot_inverse, assembled[0], preferred_element_type=jnp.float32).astype(jnp.bfloat16)
    update = jnp.dot(slab_below, pivot_solved, preferred_element_type=jnp.float32)
    below = (assembled[1].astype(jnp.float32) - update).astype(jnp.bfloat16)
    return jnp.stack([pivot_solved, below])
```

```python
import functools

import jax
import jax.numpy as jnp
from jax import lax
from jax.experimental import pallas as pl
from jax.experimental.pallas import tpu as pltpu
from jax.sharding import PartitionSpec as P

TILE = 128
VMEM_BYTES = 56 * 1024 * 1024


def largest_tile(total, most):
    best = None
    for size in range(16, most + 1, 16):
        if total % size == 0:
            best = size
    return best if best is not None else total


def front_kernel(chunk, ends, per_dest, n_col, meta_ref, tiles_ref, front_ref, *refs):
    outs, dense = refs[:n_col], refs[n_col]
    width = outs[0].shape[1]
    tile_count = tiles_ref.shape[0]
    start, stop = ends

    @pl.when(pl.program_id(0) == 0)
    def build():
        step = 512

        @pl.loop(0, dense.shape[0] // step)
        def clear(i):
            dense[pl.ds(pl.multiple_of(i * step, step), step), :] = jnp.zeros(
                (step, dense.shape[1]), dense.dtype
            )

        @pl.loop(0, tile_count)
        def place(t):
            row = meta_ref[0, t]
            dest = meta_ref[1, t]
            sub = meta_ref[2, t]

            @pl.when((sub >= start) & (sub < stop))
            def _():
                left = dest * width + (sub - start) * TILE
                dense[
                    pl.ds(pl.multiple_of(row * TILE, TILE), TILE),
                    pl.ds(pl.multiple_of(left, TILE), TILE),
                ] = tiles_ref[t]

    total = jnp.dot(front_ref[...], dense[...], preferred_element_type=jnp.float32)
    for e in range(n_col):
        outs[e][...] = total[:, e * width : (e + 1) * width].astype(outs[e].dtype)


def front_products(front, tiles, meta, start, stop, per_dest, n_col):
    rows, depth = front.shape
    width = (stop - start) * TILE
    block = largest_tile(rows, 256)
    kernel = functools.partial(front_kernel, start, (start, stop), per_dest, n_col)
    return pl.pallas_call(
        kernel,
        grid_spec=pltpu.PrefetchScalarGridSpec(
            num_scalar_prefetch=1,
            grid=(rows // block,),
            in_specs=[
                pl.BlockSpec(tiles.shape, lambda i, m: (0, 0, 0), pipeline_mode=pl.Buffered(1)),
                pl.BlockSpec((block, depth), lambda i, m: (i, 0)),
            ],
            out_specs=[pl.BlockSpec((block, width), lambda i, m: (i, 0))] * n_col,
            scratch_shapes=[pltpu.VMEM((depth, n_col * width), front.dtype)],
        ),
        out_shape=[jax.ShapeDtypeStruct((rows, width), front.dtype)] * n_col,
        compiler_params=pltpu.CompilerParams(vmem_limit_bytes=VMEM_BYTES),
        cost_estimate=pl.CostEstimate(
            flops=2 * rows * depth * n_col * width,
            bytes_accessed=2 * (rows * depth + tiles.size + rows * n_col * width),
            transcendentals=0,
        ),
        name="front_products",
    )(meta, tiles, front)


def pack_kernel(n_row, index_ref, solved_ref, *outs):
    depth = solved_ref.shape[0]
    cap = outs[0].shape[0]
    step = largest_tile(cap, 128)
    for k in range(n_row):
        for s in range(cap // step):
            want = index_ref[k * cap + s * step : k * cap + (s + 1) * step, :]
            places = lax.broadcasted_iota(jnp.int32, (step, depth), 1)
            picks = (places == want).astype(jnp.float32).astype(solved_ref.dtype)
            got = jnp.dot(picks, solved_ref[...], preferred_element_type=jnp.float32)
            outs[k][s * step : (s + 1) * step, :] = got.astype(outs[k].dtype)


def pack_rows(index, solved, n_row, cap):
    depth, width = solved.shape
    return pl.pallas_call(
        functools.partial(pack_kernel, n_row),
        out_shape=[jax.ShapeDtypeStruct((cap, width), solved.dtype)] * n_row,
        compiler_params=pltpu.CompilerParams(vmem_limit_bytes=VMEM_BYTES),
        cost_estimate=pl.CostEstimate(
            flops=2 * n_row * cap * depth * max(width, 256),
            bytes_accessed=4 * n_row * cap * width,
            transcendentals=0,
        ),
        name="pack_rows",
    )(index, solved)


def assemble_kernel(n_row, index_ref, bem_ref, *refs):
    pieces, pivot_ref, lower_ref = refs[:n_row], refs[n_row], refs[n_row + 1]
    cap = pieces[0].shape[0]
    count = pivot_ref.shape[0]
    step = largest_tile(count, 128)
    for half, out in enumerate((pivot_ref, lower_ref)):

        @pl.loop(0, count // step)
        def part(i):
            begin = pl.multiple_of(i * step, step)
            want = index_ref[pl.ds(half * count + begin, step), :]
            places = lax.broadcasted_iota(jnp.int32, (step, cap), 1)
            taken = jnp.zeros((step, out.shape[1]), jnp.float32)
            for k in range(n_row):
                picks = (places + k * cap == want).astype(jnp.float32).astype(out.dtype)
                taken = taken + jnp.dot(picks, pieces[k][...], preferred_element_type=jnp.float32)
            entries = bem_ref[half, pl.ds(begin, step), :].astype(jnp.float32)
            out[pl.ds(begin, step), :] = (entries - taken).astype(out.dtype)


def assemble(index, bem, pieces, place, n_row):
    cap, width = pieces[0].shape
    count = bem.shape[1]
    whole = lambda *shape: pl.BlockSpec(shape, lambda i: (0,) * len(shape))
    return pl.pallas_call(
        functools.partial(assemble_kernel, n_row),
        grid=(1,),
        in_specs=[
            whole(*index.shape),
            pl.BlockSpec((2, count, width), lambda i: (0, 0, place)),
        ]
        + [whole(cap, width)] * n_row,
        out_specs=[whole(count, width)] * 2,
        out_shape=[jax.ShapeDtypeStruct((count, width), bem.dtype)] * 2,
        compiler_params=pltpu.CompilerParams(vmem_limit_bytes=VMEM_BYTES),
        cost_estimate=pl.CostEstimate(
            flops=2 * 2 * count * n_row * cap * max(width, 256),
            bytes_accessed=2 * (n_row * cap + 4 * count) * width,
            transcendentals=0,
        ),
        name="assemble",
    )(index, bem, *pieces)


def route_tables(surface_map, rows, n_row, cap):
    me = lax.axis_index("row")
    mine = surface_map.reshape(-1)
    count = mine.shape[0]
    every = lax.all_gather(mine, "row")
    partners = me ^ jnp.arange(n_row, dtype=jnp.int32)
    local = every[partners] - me * rows
    asked = (local >= 0) & (local < rows)
    rank = jnp.cumsum(asked.astype(jnp.int32), axis=1) - 1
    slots = jnp.arange(cap, dtype=jnp.int32)
    hit = asked[:, None, :] & (rank[:, None, :] == slots[None, :, None])
    wanted = jnp.sum(jnp.where(hit, local[:, None, :] + 1, 0), axis=2) - 1
    owner = mine // rows
    held = owner[None, :] == jnp.arange(n_row, dtype=jnp.int32)[:, None]
    place = jnp.cumsum(held.astype(jnp.int32), axis=1) - 1
    slot = jnp.sum(jnp.where(held, place, 0), axis=0)
    lands = (owner ^ me) * cap + slot
    return wanted.reshape(n_row * cap, 1), lands.reshape(count, 1)


def add_rounded(*terms):
    total = terms[0].astype(jnp.float32)
    for term in terms[1:]:
        total = total + term.astype(jnp.float32)
    return total.astype(terms[0].dtype)


def sum_over_chain(parts, n_col):
    where = lax.axis_index("col")
    received = {}
    finals = []
    for k in range(n_col - 1):
        pairs = [(k, k + 1), (n_col - 1 - k, n_col - 2 - k)]
        for d in range(n_col - 1, k, -1):
            own = parts[d if k < n_col // 2 else n_col - 1 - d]
            value = own if k == 0 else add_rounded(own, received[k - 1, d])
            received[k, d] = lax.ppermute(value, "col", pairs)
        finals.append(received[k, k + 1])
    own = parts[0]
    for e in range(1, n_col // 2):
        own = jnp.where(jnp.minimum(where, n_col - 1 - where) == e, parts[e], own)
    return add_rounded(own, *finals)


def per_device(
    front_inverse,
    coupling_tiles,
    tile_row,
    tile_col,
    surface_map,
    bem_entries,
    pivot_inverse,
    slab_below,
):
    n_row, n_col = lax.axis_size("row"), lax.axis_size("col")
    assert n_row & (n_row - 1) == 0 and n_col % 2 == 0
    rows, depth = front_inverse.shape
    per_dest = bem_entries.shape[2] // TILE
    cap = rows // n_row
    col_at = lax.axis_index("col")

    dest = tile_col // per_dest
    mirrored = jnp.where(col_at < n_col // 2, dest, n_col - 1 - dest)
    meta = jnp.stack([tile_row - col_at * (depth // TILE), mirrored, tile_col % per_dest])
    wanted, lands = route_tables(surface_map, rows, n_row, cap)

    pivots, belows = [], []
    for chunk in range(per_dest):
        parts = front_products(
            front_inverse, coupling_tiles, meta, chunk, chunk + 1, per_dest, n_col
        )
        solved = sum_over_chain(parts, n_col)
        packed = pack_rows(wanted, solved, n_row, cap)
        pieces = [packed[0]]
        for k in range(1, n_row):
            pairs = [(i, i ^ k) for i in range(n_row)]
            pieces.append(lax.ppermute(packed[k], "row", pairs))
        upper, lower = assemble(lands, bem_entries, pieces, chunk, n_row)
        gathered = lax.all_gather(upper, "row", axis=0, tiled=True)
        pivot = jnp.dot(pivot_inverse, gathered, preferred_element_type=jnp.float32)
        pivot = pivot.astype(jnp.bfloat16)
        update = jnp.dot(
            slab_below,
            lax.all_gather(pivot, "row", axis=0, tiled=True),
            preferred_element_type=jnp.float32,
        )
        pivots.append(pivot)
        belows.append((lower.astype(jnp.float32) - update).astype(jnp.bfloat16))
    return jnp.stack([jnp.concatenate(pivots, axis=1), jnp.concatenate(belows, axis=1)])


def solution(mesh):
    placed = (
        P("row", "col"),
        P("col", None, None),
        P("col"),
        P("col"),
        P(None, "row"),
        P(None, "row", "col"),
        P("row", None),
        P("row", None),
    )
    return jax.shard_map(
        per_device, mesh=mesh, in_specs=placed, out_specs=P(None, "row", "col"), check_vma=False
    )
```

```python
import functools

import jax
import jax.numpy as jnp
from jax import lax
from jax.experimental import pallas as pl
from jax.experimental.pallas import tpu as pltpu
from jax.sharding import PartitionSpec as P

TILE = 128
STACK = 4
VMEM_BYTES = 56 * 1024 * 1024


def largest_tile(total, most):
    best = total
    for size in range(16, most + 1, 16):
        if total % size == 0:
            best = size
    return best


def kernel_params():
    return pltpu.CompilerParams(vmem_limit_bytes=VMEM_BYTES)


def whole_block(*shape):
    return pl.BlockSpec(shape, lambda *_: (0,) * len(shape))


def dot32(left, right):
    return jnp.dot(left, right, preferred_element_type=jnp.float32)


def front_kernel(start, stop, n_col, flat, meta_ref, tiles_ref, front_ref, out_ref, stack, acc, rows_of, count):
    span = stop - start
    groups = n_col * span

    @pl.when(pl.program_id(0) == 0)
    def build():
        for g in range(groups):
            count[g] = 0

        @pl.loop(0, tiles_ref.shape[0])
        def place(t):
            sub = meta_ref[2, t]

            @pl.when((sub >= start) & (sub < stop))
            def _():
                g = meta_ref[1, t] * span + sub - start
                at = count[g]
                rows_of[g, at] = meta_ref[0, t]
                stack[g, pl.ds(pl.multiple_of(at * TILE, TILE), TILE), :] = tiles_ref[t]
                count[g] = at + 1

        for g in range(groups):
            used = count[g]
            padded = (used + STACK - 1) // STACK * STACK

            @pl.loop(used, padded)
            def fill(at):
                rows_of[g, at] = 0
                stack[g, pl.ds(pl.multiple_of(at * TILE, TILE), TILE), :] = jnp.zeros(
                    (TILE, TILE), stack.dtype
                )

    for g in range(groups):
        acc[...] = jnp.zeros_like(acc)

        @pl.loop(0, (count[g] + STACK - 1) // STACK)
        def add(s):
            pieces = []
            for j in range(STACK):
                left = pl.multiple_of(rows_of[g, s * STACK + j] * TILE, TILE)
                pieces.append(front_ref[:, pl.ds(left, TILE)])
            deep = STACK * TILE
            tiles = stack[g, pl.ds(pl.multiple_of(s * deep, deep), deep), :]
            acc[...] += dot32(jnp.concatenate(pieces, axis=1), tiles)

        dest, sub = g // span, g % span
        if flat:
            out_ref[:, g * TILE : (g + 1) * TILE] = acc[...].astype(out_ref.dtype)
        else:
            out_ref[dest, :, sub * TILE : (sub + 1) * TILE] = acc[...].astype(out_ref.dtype)


def front_products(front, tiles, meta, start, stop, n_col, flat):
    rows, depth = front.shape
    span = stop - start
    width = span * TILE
    block = largest_tile(rows, 512)
    deepest = -(-depth // (TILE * STACK)) * STACK
    if flat:
        shape, spec = (rows, n_col * width), pl.BlockSpec((block, n_col * width), lambda i, m: (i, 0))
    else:
        shape, spec = (n_col, rows, width), pl.BlockSpec((n_col, block, width), lambda i, m: (0, i, 0))
    return pl.pallas_call(
        functools.partial(front_kernel, start, stop, n_col, flat),
        grid_spec=pltpu.PrefetchScalarGridSpec(
            num_scalar_prefetch=1,
            grid=(rows // block,),
            in_specs=[
                pl.BlockSpec(tiles.shape, lambda i, m: (0, 0, 0), pipeline_mode=pl.Buffered(1)),
                pl.BlockSpec((block, depth), lambda i, m: (i, 0)),
            ],
            out_specs=spec,
            scratch_shapes=[
                pltpu.VMEM((n_col * span, deepest * TILE, TILE), front.dtype),
                pltpu.VMEM((block, TILE), jnp.float32),
                pltpu.SMEM((n_col * span, deepest), jnp.int32),
                pltpu.SMEM((n_col * span,), jnp.int32),
            ],
        ),
        out_shape=jax.ShapeDtypeStruct(shape, front.dtype),
        compiler_params=kernel_params(),
        cost_estimate=pl.CostEstimate(
            flops=rows * depth * n_col * width,
            bytes_accessed=2 * (rows * depth + tiles.size + rows * n_col * width),
            transcendentals=0,
        ),
        name="front_products",
    )(meta, tiles, front)


def one_hot(want, depth, kind):
    places = lax.broadcasted_iota(jnp.int32, (want.shape[0], depth), 1)
    return (places == want).astype(jnp.float32).astype(kind)


def pack_kernel(n_row, index_ref, solved_ref, *outs):
    cap = outs[0].shape[0]
    for k in range(n_row):
        picks = one_hot(index_ref[k * cap : (k + 1) * cap, :], solved_ref.shape[0], solved_ref.dtype)
        outs[k][...] = dot32(picks, solved_ref[...]).astype(outs[k].dtype)


def pack_rows(index, solved, n_row, cap):
    depth, width = solved.shape
    return pl.pallas_call(
        functools.partial(pack_kernel, n_row),
        out_shape=[jax.ShapeDtypeStruct((cap, width), solved.dtype)] * n_row,
        compiler_params=kernel_params(),
        cost_estimate=pl.CostEstimate(
            flops=2 * n_row * cap * depth * max(width, 256),
            bytes_accessed=4 * n_row * cap * width,
            transcendentals=0,
        ),
        name="pack_rows",
    )(index, solved)


def join_pieces(pieces, joined):
    cap = pieces[0].shape[0]
    for k, piece in enumerate(pieces):
        joined[k * cap : (k + 1) * cap, :] = piece[...]


def assemble_kernel(n_row, index_ref, bem_ref, *refs):
    outs, joined = refs[n_row : n_row + 2], refs[n_row + 2]
    join_pieces(refs[:n_row], joined)
    count = outs[0].shape[0]
    step = largest_tile(count, 512)
    for half, out in enumerate(outs):
        for i in range(0, count, step):
            want = index_ref[half * count + i : half * count + i + step, :]
            taken = dot32(one_hot(want, joined.shape[0], joined.dtype), joined[...])
            entries = bem_ref[half, i : i + step, :].astype(jnp.float32)
            out[i : i + step, :] = (entries - taken).astype(out.dtype)


def assemble(index, bem, pieces, start, n_row):
    cap, width = pieces[0].shape
    count = bem.shape[1]
    place = start * TILE // width
    return pl.pallas_call(
        functools.partial(assemble_kernel, n_row),
        grid=(1,),
        in_specs=[
            whole_block(*index.shape),
            pl.BlockSpec((2, count, width), lambda i: (0, 0, place)),
        ]
        + [whole_block(cap, width)] * n_row,
        out_specs=[whole_block(count, width)] * 2,
        out_shape=[jax.ShapeDtypeStruct((count, width), bem.dtype)] * 2,
        scratch_shapes=[pltpu.VMEM((n_row * cap, width), bem.dtype)],
        compiler_params=kernel_params(),
        cost_estimate=pl.CostEstimate(
            flops=2 * 2 * count * n_row * cap * max(width, 256),
            bytes_accessed=2 * (n_row * cap + 4 * count) * width,
            transcendentals=0,
        ),
        name="assemble",
    )(index, bem, *pieces)


def unpack_kernel(n_row, index_ref, *refs):
    out, joined = refs[n_row], refs[n_row + 1]
    join_pieces(refs[:n_row], joined)
    n_col, count, width = out.shape
    step = largest_tile(count, 512)
    for i in range(0, count, step):
        taken = dot32(one_hot(index_ref[i : i + step, :], joined.shape[0], joined.dtype), joined[...])
        for d in range(n_col):
            out[d, i : i + step, :] = taken[:, d * width : (d + 1) * width].astype(out.dtype)


def unpack(index, pieces, n_row, n_col):
    cap, wide = pieces[0].shape
    count, width = index.shape[0], wide // n_col
    return pl.pallas_call(
        functools.partial(unpack_kernel, n_row),
        out_shape=jax.ShapeDtypeStruct((n_col, count, width), pieces[0].dtype),
        scratch_shapes=[pltpu.VMEM((n_row * cap, wide), pieces[0].dtype)],
        compiler_params=kernel_params(),
        cost_estimate=pl.CostEstimate(
            flops=2 * count * n_row * cap * wide,
            bytes_accessed=2 * (n_row * cap + count) * wide,
            transcendentals=0,
        ),
        name="unpack",
    )(index, *pieces)


def product_kernel(minus, order_ref, matrix_ref, near_ref, far_ref, *refs):
    base_ref, out_ref, acc = refs if minus else (None, *refs)
    k = pl.program_id(0)
    steps = pl.num_programs(0)
    half = steps // 2
    deep = matrix_ref.shape[1]

    @pl.when(k == 0)
    def _():
        acc[...] = dot32(matrix_ref[...], near_ref[pl.ds(0, deep), :])

    @pl.when((k > 0) & (k < half))
    def _():
        at = pl.multiple_of(k * deep, deep)
        acc[...] += dot32(matrix_ref[...], near_ref[pl.ds(at, deep), :])

    @pl.when(k >= half)
    def _():
        at = pl.multiple_of((k - half) * deep, deep)
        acc[...] += dot32(matrix_ref[...], far_ref[pl.ds(at, deep), :])

    @pl.when(k == steps - 1)
    def _():
        total = acc[...]
        if minus:
            total = base_ref[...].astype(jnp.float32) - total
        out_ref[...] = total.astype(out_ref.dtype)


def product(matrix, order, near, far, base=None):
    rows, depth = matrix.shape
    width = near.shape[1]
    n_row = order.shape[0]
    deep = depth // n_row
    bases = [] if base is None else [base]
    return pl.pallas_call(
        functools.partial(product_kernel, bool(bases)),
        grid_spec=pltpu.PrefetchScalarGridSpec(
            num_scalar_prefetch=1,
            grid=(n_row,),
            in_specs=[pl.BlockSpec((rows, deep), lambda k, order: (0, order[k]))]
            + [whole_block(*near.shape)] * 2
            + [whole_block(rows, width)] * len(bases),
            out_specs=whole_block(rows, width),
            scratch_shapes=[pltpu.VMEM((rows, width), jnp.float32)],
        ),
        out_shape=jax.ShapeDtypeStruct((rows, width), near.dtype),
        compiler_params=kernel_params(),
        cost_estimate=pl.CostEstimate(
            flops=2 * rows * depth * max(width, 256),
            bytes_accessed=2 * (rows * depth + (depth + 2 * rows) * width),
            transcendentals=0,
        ),
        name="product",
    )(order, matrix, near, far, *bases)


def exchange(value, distance, n_row):
    return lax.ppermute(value, "row", [(i, i ^ distance) for i in range(n_row)])


def route(packed, n_row):
    return [packed[0]] + [exchange(packed[k], k, n_row) for k in range(1, n_row)]


def gather_rows(block, n_row):
    near = [block] + [exchange(block, k, n_row) for k in range(2, n_row, 2)]
    near = jnp.concatenate(near, axis=0)
    return near, exchange(near, 1, n_row)


def route_tables(surface_map, rows, n_row, cap, slots):
    me = lax.axis_index("row")
    mine = surface_map.reshape(-1)
    every = lax.all_gather(mine, "row")
    partners = me ^ jnp.arange(n_row, dtype=jnp.int32)
    local = every[partners] - me * rows
    asked = (local >= 0) & (local < rows)
    rank = jnp.cumsum(asked.astype(jnp.int32), axis=1) - 1
    numbers = jnp.arange(slots, dtype=jnp.int32)
    hit = asked[:, None, :] & (rank[:, None, :] == numbers[None, :, None])
    wanted = jnp.sum(jnp.where(hit, local[:, None, :] + 1, 0), axis=2) - 1
    owner = mine // rows
    held = owner[None, :] == jnp.arange(n_row, dtype=jnp.int32)[:, None]
    place = jnp.cumsum(held.astype(jnp.int32), axis=1) - 1
    slot = jnp.sum(jnp.where(held, place, 0), axis=0)
    lands = (owner ^ me) * slots + slot
    return wanted.reshape(-1, 1), lands.reshape(-1, 1)


def per_device(
    front_inverse,
    coupling_tiles,
    tile_row,
    tile_col,
    surface_map,
    bem_entries,
    pivot_inverse,
    slab_below,
):
    n_row, n_col = lax.axis_size("row"), lax.axis_size("col")
    assert n_row > 1 and n_row & (n_row - 1) == 0
    rows, depth = front_inverse.shape
    count = bem_entries.shape[1]
    per_dest = bem_entries.shape[2] // TILE
    cap = rows // n_row
    slots = -(-cap // 16) * 16
    me = lax.axis_index("row")

    meta = jnp.stack(
        [tile_row - lax.axis_index("col") * (depth // TILE), tile_col // per_dest, tile_col % per_dest]
    )
    order = me ^ jnp.concatenate(
        [jnp.arange(0, n_row, 2, dtype=jnp.int32), jnp.arange(1, n_row, 2, dtype=jnp.int32)]
    )
    half = per_dest // 2
    first = front_products(front_inverse, coupling_tiles, meta, 0, half, n_col, False)
    first = lax.psum_scatter(first, "col", scatter_dimension=0)
    wanted, lands = route_tables(surface_map, rows, n_row, cap, slots)

    later = []
    for start in range(half, per_dest):
        parts = front_products(
            front_inverse, coupling_tiles, meta, start, start + 1, n_col, True
        )
        pieces = route(pack_rows(wanted, parts, n_row, slots), n_row)
        parts = unpack(lands, pieces, n_row, n_col)
        later.append(lax.psum_scatter(parts, "col", scatter_dimension=0))

    pieces = route(pack_rows(wanted, first, n_row, slots), n_row)
    assembled = [assemble(lands, bem_entries, pieces, 0, n_row)]
    for start, schur in zip(range(half, per_dest), later):
        entries = bem_entries[:, :, start * TILE : (start + 1) * TILE].astype(jnp.float32)
        both = entries - schur.reshape(2, count, TILE).astype(jnp.float32)
        both = both.astype(bem_entries.dtype)
        assembled.append((both[0], both[1]))

    pivots, belows = [], []
    for upper, lower in assembled:
        pivot = product(pivot_inverse, order, *gather_rows(upper, n_row))
        pivots.append(pivot)
        belows.append(product(slab_below, order, *gather_rows(pivot, n_row), lower))
    return jnp.stack([jnp.concatenate(pivots, axis=1), jnp.concatenate(belows, axis=1)])


def solution(mesh):
    placed = (
        P("row", "col"),
        P("col", None, None),
        P("col"),
        P("col"),
        P(None, "row"),
        P(None, "row", "col"),
        P("row", None),
        P("row", None),
    )
    return jax.shard_map(
        per_device, mesh=mesh, in_specs=placed, out_specs=P(None, "row", "col"), check_vma=False
    )
```

```python
import functools

import jax
import jax.numpy as jnp
from jax import lax
from jax.experimental import pallas as pl
from jax.experimental.pallas import tpu as pltpu
from jax.sharding import PartitionSpec as P

TILE = 128
STACK = 4
VMEM_BYTES = 56 * 1024 * 1024


def largest_tile(total, most):
    best = total
    for size in range(16, most + 1, 16):
        if total % size == 0:
            best = size
    return best


def kernel_params():
    return pltpu.CompilerParams(vmem_limit_bytes=VMEM_BYTES)


def brief():
    return pl.CostEstimate(flops=1, bytes_accessed=1, transcendentals=0)


def whole_block(*shape):
    return pl.BlockSpec(shape, lambda *_: (0,) * len(shape))


def in_place():
    return pl.BlockSpec(memory_space=pl.ANY)


def dot32(left, right):
    return jnp.dot(left, right, preferred_element_type=jnp.float32)


def front_kernel(start, stop, n_col, flat, n_after, meta_ref, tiles_ref, front_ref, *refs):
    out_ref, stack, held, acc, places, groups_of, state, tile_sems, sems = refs[n_after:]
    span = stop - start
    groups = n_col * span
    block, streams = held.shape[1], sems.shape[1]
    lines = block // streams
    step = pl.program_id(0)
    slot = lax.rem(step, 2)

    def front_copy(at, into, q):
        return pltpu.make_async_copy(
            front_ref.at[pl.ds(pl.multiple_of(at * block + q * lines, lines), lines), :],
            held.at[into, pl.ds(q * lines, lines), :],
            sems.at[into, q],
        )

    def tile_copy(t, item, place):
        return pltpu.make_async_copy(
            tiles_ref.at[t],
            stack.at[item, pl.ds(pl.multiple_of(place * TILE, TILE), TILE), :],
            tile_sems.at[t],
        )

    def chosen(t):
        return (meta_ref[2, t] >= start) & (meta_ref[2, t] < stop)

    def clear(item, place):
        places[item, place] = 0
        stack[item, pl.ds(pl.multiple_of(place * TILE, TILE), TILE), :] = jnp.zeros(
            (TILE, TILE), stack.dtype
        )

    @pl.when(step == 0)
    def build():
        for q in range(streams):
            front_copy(0, 0, q).start()
        for g in range(groups):
            state[g] = 0
            state[groups + g] = 0
        state[2 * groups] = 0

        @pl.loop(0, tiles_ref.shape[0])
        def place_tile(t):
            @pl.when(chosen(t))
            def _():
                g = meta_ref[1, t] * span + meta_ref[2, t] - start
                at = state[g]

                @pl.when(lax.rem(at, STACK) == 0)
                def _():
                    state[groups + g] = state[2 * groups]
                    groups_of[state[2 * groups]] = g
                    state[2 * groups] += 1

                item = state[groups + g]
                places[item, lax.rem(at, STACK)] = meta_ref[0, t]
                tile_copy(t, item, lax.rem(at, STACK)).start()
                state[g] = at + 1

        for g in range(groups):
            used = lax.rem(state[g], STACK)

            @pl.loop(used, jnp.where(used == 0, 0, STACK))
            def fill(place):
                clear(state[groups + g], place)

        items = state[2 * groups]

        @pl.loop(items, (items + STACK - 1) // STACK * STACK)
        def fill_item(item):
            groups_of[item] = 0
            for place in range(STACK):
                clear(item, place)

        @pl.loop(0, tiles_ref.shape[0])
        def wait_tile(t):
            @pl.when(chosen(t))
            def _():
                tile_copy(t, 0, 0).wait()

    @pl.when(step + 1 < pl.num_programs(0))
    def ahead():
        for q in range(streams):
            front_copy(step + 1, 1 - slot, q).start()

    for q in range(streams):
        front_copy(step, slot, q).wait()

    acc[...] = jnp.zeros_like(acc)

    @pl.loop(0, (state[2 * groups] + STACK - 1) // STACK)
    def add(s):
        products = []
        for i in range(STACK):
            item = s * STACK + i
            lefts = [pl.multiple_of(places[item, j] * TILE, TILE) for j in range(STACK)]
            rows = [held[slot, :, pl.ds(left, TILE)] for left in lefts]
            products.append(dot32(jnp.concatenate(rows, axis=1), stack[item]))
        for i in range(STACK):
            acc[groups_of[s * STACK + i]] += products[i]

    for g in range(groups):
        dest, sub = g // span, g % span
        if flat:
            out_ref[:, g * TILE : (g + 1) * TILE] = acc[g].astype(out_ref.dtype)
        else:
            out_ref[dest, :, sub * TILE : (sub + 1) * TILE] = acc[g].astype(out_ref.dtype)


def front_products(front, tiles, meta, start, stop, n_col, flat, after=()):
    rows, depth = front.shape
    span = stop - start
    width = span * TILE
    groups = n_col * span
    block = largest_tile(rows, 512)
    streams = 8 if block % 128 == 0 else 1
    count = tiles.shape[0]
    items = (-(-count // STACK) + groups + STACK) // STACK * STACK
    if flat:
        shape, spec = (rows, n_col * width), pl.BlockSpec((block, n_col * width), lambda i, m: (i, 0))
    else:
        shape, spec = (n_col, rows, width), pl.BlockSpec((n_col, block, width), lambda i, m: (0, i, 0))
    return pl.pallas_call(
        functools.partial(front_kernel, start, stop, n_col, flat, len(after)),
        grid_spec=pltpu.PrefetchScalarGridSpec(
            num_scalar_prefetch=1,
            grid=(rows // block,),
            in_specs=[in_place()] * (2 + len(after)),
            out_specs=spec,
            scratch_shapes=[
                pltpu.VMEM((items, STACK * TILE, TILE), front.dtype),
                pltpu.VMEM((2, block, depth), front.dtype),
                pltpu.VMEM((groups, block, TILE), jnp.float32),
                pltpu.SMEM((items, STACK), jnp.int32),
                pltpu.SMEM((items,), jnp.int32),
                pltpu.SMEM((2 * groups + 1,), jnp.int32),
                pltpu.SemaphoreType.DMA((count,)),
                pltpu.SemaphoreType.DMA((2, streams)),
            ],
        ),
        out_shape=jax.ShapeDtypeStruct(shape, front.dtype),
        compiler_params=kernel_params(),
        cost_estimate=brief(),
        name="front_products",
    )(meta, tiles, front, *after)


def one_hot(want, depth, kind):
    places = lax.broadcasted_iota(jnp.int32, (want.shape[0], depth), 1)
    return (places == want).astype(jnp.float32).astype(kind)


def pack_kernel(n_row, n_solved, index_ref, *refs):
    outs = refs[-2:]
    solved = jnp.concatenate([ref[...] for ref in refs[:n_solved]], axis=1)
    cap = outs[0].shape[0] * 2 // n_row
    for k in range(n_row):
        picks = one_hot(index_ref[k * cap : (k + 1) * cap, :], solved.shape[0], solved.dtype)
        at = k // 2 * cap
        outs[k % 2][at : at + cap, :] = dot32(picks, solved).astype(outs[0].dtype)


def pack_rows(index, solved, n_row, cap, after=()):
    depth = solved[0].shape[0]
    width = sum(part.shape[1] for part in solved)
    return pl.pallas_call(
        functools.partial(pack_kernel, n_row, len(solved)),
        in_specs=[whole_block(*index.shape)]
        + [whole_block(*part.shape) for part in solved]
        + [in_place()] * len(after),
        out_shape=[jax.ShapeDtypeStruct((n_row // 2 * cap, width), solved[0].dtype)] * 2,
        compiler_params=kernel_params(),
        cost_estimate=brief(),
        name="pack_rows",
    )(index, *solved, *after)


def join_pieces(pieces, joined):
    at = 0
    for piece in pieces:
        joined[at : at + piece.shape[0], :] = piece[...]
        at += piece.shape[0]


def assemble_kernel(n_pieces, index_ref, bem_ref, *refs):
    outs, joined = refs[-3:-1], refs[-1]
    join_pieces(refs[:n_pieces], joined)
    count = outs[0].shape[0]
    step = largest_tile(count, 512)
    for half, out in enumerate(outs):
        for i in range(0, count, step):
            want = index_ref[half * count + i : half * count + i + step, :]
            taken = dot32(one_hot(want, joined.shape[0], joined.dtype), joined[...])
            entries = bem_ref[half, i : i + step, :].astype(jnp.float32)
            out[i : i + step, :] = (entries - taken).astype(out.dtype)


def assemble(index, bem, pieces, start, after=()):
    width = pieces[0].shape[1]
    routed = sum(piece.shape[0] for piece in pieces)
    count = bem.shape[1]
    place = start * TILE // width
    return pl.pallas_call(
        functools.partial(assemble_kernel, len(pieces)),
        grid=(1,),
        in_specs=[
            whole_block(*index.shape),
            pl.BlockSpec((2, count, width), lambda i: (0, 0, place)),
        ]
        + [whole_block(*piece.shape) for piece in pieces]
        + [in_place()] * len(after),
        out_specs=[whole_block(count, width)] * 2,
        out_shape=[jax.ShapeDtypeStruct((count, width), bem.dtype)] * 2,
        scratch_shapes=[pltpu.VMEM((routed, width), bem.dtype)],
        compiler_params=kernel_params(),
        cost_estimate=brief(),
        name="assemble",
    )(index, bem, *pieces, *after)


def subtract_kernel(bem_ref, terms_ref, *refs):
    for half, out in enumerate(refs[-2:]):
        total = terms_ref[0, half].astype(jnp.float32)
        for term in range(1, terms_ref.shape[0]):
            total = total + terms_ref[term, half].astype(jnp.float32)
        taken = total.astype(out.dtype).astype(jnp.float32)
        out[...] = (bem_ref[half].astype(jnp.float32) - taken).astype(out.dtype)


def subtract(bem, terms, start, after=()):
    count, width = bem.shape[1], terms.shape[1]
    place = start * TILE // width
    return pl.pallas_call(
        subtract_kernel,
        grid=(1,),
        in_specs=[pl.BlockSpec((2, count, width), lambda i: (0, 0, place))]
        + [whole_block(1, 2, count, width)]
        + [in_place()] * len(after),
        out_specs=[whole_block(count, width)] * 2,
        out_shape=[jax.ShapeDtypeStruct((count, width), bem.dtype)] * 2,
        compiler_params=kernel_params(),
        cost_estimate=brief(),
        name="subtract",
    )(bem, terms.reshape(1, 2, count, width), *after)


def unpack_kernel(n_pieces, n_col, index_ref, *refs):
    out, joined = refs[-2:]
    join_pieces(refs[:n_pieces], joined)
    _, count, width = out.shape
    step = largest_tile(count, 512)
    for i in range(0, count, step):
        taken = dot32(one_hot(index_ref[i : i + step, :], joined.shape[0], joined.dtype), joined[...])
        for d in range(n_col):
            out[d, i : i + step, :] = taken[:, d * width : (d + 1) * width].astype(out.dtype)


def unpack(index, pieces, n_col, after=()):
    wide = pieces[0].shape[1]
    routed = sum(piece.shape[0] for piece in pieces)
    count, width = index.shape[0], wide // n_col
    return pl.pallas_call(
        functools.partial(unpack_kernel, len(pieces), n_col),
        in_specs=[whole_block(*index.shape)]
        + [whole_block(*piece.shape) for piece in pieces]
        + [in_place()] * len(after),
        out_shape=jax.ShapeDtypeStruct((n_col, count, width), pieces[0].dtype),
        scratch_shapes=[pltpu.VMEM((routed, wide), pieces[0].dtype)],
        compiler_params=kernel_params(),
        cost_estimate=brief(),
        name="unpack",
    )(index, *pieces, *after)


def product_kernel(streams, minus, order_ref, *refs):
    blocks, (near_ref, far_ref) = refs[:streams], refs[streams : streams + 2]
    out_ref, acc = refs[-2:]
    k = pl.program_id(0)
    steps = pl.num_programs(0)
    half = steps // 2
    deep = near_ref.shape[0] // half

    def term(rows_ref, at):
        matrix = jnp.concatenate([block[...] for block in blocks], axis=1)
        return dot32(matrix, rows_ref[pl.ds(pl.multiple_of(at * deep, deep), deep), :])

    @pl.when(k == 0)
    def _():
        acc[...] = term(near_ref, 0)

    @pl.when((k > 0) & (k < half))
    def _():
        acc[...] += term(near_ref, k)

    @pl.when(k >= half)
    def _():
        acc[...] += term(far_ref, k - half)

    @pl.when(k == steps - 1)
    def _():
        total = acc[...]
        if minus:
            total = refs[streams + 2][...].astype(jnp.float32) - total
        out_ref[...] = total.astype(out_ref.dtype)


def product(matrix, order, near, far, base=None, after=()):
    rows, depth = matrix.shape
    width = near.shape[1]
    n_row = order.shape[0]
    deep = depth // n_row
    streams = 4 if deep % (4 * TILE) == 0 else 1
    bases = [] if base is None else [base]

    def block_of(q):
        return pl.BlockSpec((rows, deep // streams), lambda k, order: (0, order[k] * streams + q))

    return pl.pallas_call(
        functools.partial(product_kernel, streams, bool(bases)),
        grid_spec=pltpu.PrefetchScalarGridSpec(
            num_scalar_prefetch=1,
            grid=(n_row,),
            in_specs=[block_of(q) for q in range(streams)]
            + [whole_block(*near.shape)] * 2
            + [whole_block(rows, width)] * len(bases)
            + [in_place()] * len(after),
            out_specs=whole_block(rows, width),
            scratch_shapes=[pltpu.VMEM((rows, width), jnp.float32)],
        ),
        out_shape=jax.ShapeDtypeStruct((rows, width), near.dtype),
        compiler_params=kernel_params(),
        cost_estimate=brief(),
        name="product",
    )(order, *[matrix] * streams, near, far, *bases, *after)


def exchange(value, distance, n, axis="row"):
    return lax.ppermute(value, axis, [(i, i ^ distance) for i in range(n)])


def route(packed, n_row):
    near, far = packed[0], exchange(packed[1], 1, n_row)
    cap = near.shape[0] * 2 // n_row
    pieces = [near[:cap], far[:cap]]
    for i in range(1, n_row // 2):
        both = [near[i * cap : (i + 1) * cap], far[i * cap : (i + 1) * cap]]
        pieces.append(exchange(jnp.concatenate(both, axis=0), 2 * i, n_row))
    return pieces


def gather_rows(block, n_row):
    near = [block] + [exchange(block, k, n_row) for k in range(2, n_row, 2)]
    near = jnp.concatenate(near, axis=0)
    return near, exchange(near, 1, n_row)


def route_tables(surface_map, rows, n_row, cap, slots):
    me = lax.axis_index("row")
    mine = surface_map.reshape(-1)
    every = lax.all_gather(mine, "row")
    partners = me ^ jnp.arange(n_row, dtype=jnp.int32)
    local = every[partners] - me * rows
    asked = (local >= 0) & (local < rows)
    rank = jnp.cumsum(asked.astype(jnp.int32), axis=1) - 1
    numbers = jnp.arange(slots, dtype=jnp.int32)
    hit = asked[:, None, :] & (rank[:, None, :] == numbers[None, :, None])
    wanted = jnp.sum(jnp.where(hit, local[:, None, :] + 1, 0), axis=2) - 1
    owner = mine // rows
    held = owner[None, :] == jnp.arange(n_row, dtype=jnp.int32)[:, None]
    place = jnp.cumsum(held.astype(jnp.int32), axis=1) - 1
    slot = jnp.sum(jnp.where(held, place, 0), axis=0)
    lands = (owner ^ me) * slots + slot
    return wanted.reshape(-1, 1), lands.reshape(-1, 1)


def per_device(
    front_inverse,
    coupling_tiles,
    tile_row,
    tile_col,
    surface_map,
    bem_entries,
    pivot_inverse,
    slab_below,
):
    n_row, n_col = lax.axis_size("row"), lax.axis_size("col")
    assert n_row > 1 and n_row & (n_row - 1) == 0
    rows, depth = front_inverse.shape
    count = bem_entries.shape[1]
    per_dest = bem_entries.shape[2] // TILE
    cap = rows // n_row
    slots = -(-cap // 16) * 16
    me = lax.axis_index("row")

    col_at = lax.axis_index("col")
    block_row = tile_row - col_at * (depth // TILE)
    dest, sub = tile_col // per_dest, tile_col % per_dest
    meta = jnp.stack([block_row, dest, sub])
    order = me ^ jnp.concatenate(
        [jnp.arange(0, n_row, 2, dtype=jnp.int32), jnp.arange(1, n_row, 2, dtype=jnp.int32)]
    )
    half = per_dest // 2

    def front_of(start, flat, after):
        return front_products(
            front_inverse, coupling_tiles, meta, start, start + 1, n_col, flat, after
        )

    def summed(parts):
        return lax.psum_scatter(parts, "col", scatter_dimension=0)

    solved, after = [], ()
    for start in range(half):
        parts = front_of(start, False, after)
        after = (parts,)
        solved.append(summed(parts))

    wanted, lands = route_tables(surface_map, rows, n_row, cap, slots)
    routed = []
    for start in range(half, per_dest):
        parts = front_of(start, True, after)
        packed = pack_rows(wanted, [parts], n_row, slots)
        after = (packed[0],)
        routed.append(route(packed, n_row))
    schur = []
    for pieces in routed:
        parts = unpack(lands, pieces, n_col, after)
        schur.append(summed(parts))
        if len(schur) == 1:
            packed = pack_rows(wanted, solved, n_row, slots, (parts,))
            after = (packed[0],)

    def blocks_of(g):
        after = (last,)
        if g == 0:
            return assemble(lands, bem_entries, route(packed, n_row), 0, after)
        return subtract(bem_entries, schur[g - 1], half + g - 1, after)

    sequence = list(range(1 + per_dest - half))
    last = parts
    lowers, gathered = {}, {}
    for g in sequence:
        last, lowers[g] = blocks_of(g)
        gathered[g] = gather_rows(last, n_row)
    pivots, belows = {}, {}
    for g in sequence:
        last = pivots[g] = product(pivot_inverse, order, *gathered[g], after=(last,))
        gathered[g] = gather_rows(last, n_row)
    for g in sequence:
        last = belows[g] = product(slab_below, order, *gathered[g], lowers[g], (last,))
    return jnp.stack(
        [jnp.concatenate([part[g] for g in sorted(part)], axis=1) for part in (pivots, belows)]
    )


def solution(mesh):
    placed = (
        P("row", "col"),
        P("col", None, None),
        P("col"),
        P("col"),
        P(None, "row"),
        P(None, "row", "col"),
        P("row", None),
        P("row", None),
    )
    return jax.shard_map(
        per_device, mesh=mesh, in_specs=placed, out_specs=P(None, "row", "col"), check_vma=False
    )
```

```python
import functools

import jax
import jax.numpy as jnp
from jax import lax
from jax.experimental import pallas as pl
from jax.experimental.pallas import tpu as pltpu
from jax.sharding import PartitionSpec as P

TILE = 128
STACK = 4
VMEM_BYTES = 56 * 1024 * 1024


def largest_tile(total, most):
    best = total
    for size in range(16, most + 1, 16):
        if total % size == 0:
            best = size
    return best


def kernel_params():
    return pltpu.CompilerParams(vmem_limit_bytes=VMEM_BYTES)


def declared(flops=0):
    return pl.CostEstimate(flops=flops, bytes_accessed=1, transcendentals=0)


def whole_block(*shape):
    return pl.BlockSpec(shape, lambda *_: (0,) * len(shape))


def in_place():
    return pl.BlockSpec(memory_space=pl.ANY)


def dot32(left, right):
    return jnp.dot(left, right, preferred_element_type=jnp.float32)


def front_kernel(subs, flats, n_col, n_after, meta_ref, tiles_ref, front_ref, *refs):
    outs = refs[n_after : n_after + len(subs)]
    stack, held, acc, places, groups_of, state, tile_sems, sems = refs[n_after + len(subs) :]
    groups = n_col * len(subs)
    block, streams = held.shape[1], sems.shape[1]
    lines = block // streams
    step = pl.program_id(0)
    slot = lax.rem(step, 2)

    def front_copy(at, into, q):
        return pltpu.make_async_copy(
            front_ref.at[pl.ds(pl.multiple_of(at * block + q * lines, lines), lines), :],
            held.at[into, pl.ds(q * lines, lines), :],
            sems.at[into, q],
        )

    def tile_copy(t, item, place):
        return pltpu.make_async_copy(
            tiles_ref.at[t],
            stack.at[item, pl.ds(pl.multiple_of(place * TILE, TILE), TILE), :],
            tile_sems.at[t],
        )

    def chosen(t):
        return functools.reduce(jnp.logical_or, [meta_ref[2, t] == sub for sub in subs])

    def group_of(t):
        order = 0
        for p in range(1, len(subs)):
            order = jnp.where(meta_ref[2, t] == subs[p], p, order)
        return order * n_col + meta_ref[1, t]

    def clear(item, place):
        places[item, place] = 0
        stack[item, pl.ds(pl.multiple_of(place * TILE, TILE), TILE), :] = jnp.zeros(
            (TILE, TILE), stack.dtype
        )

    @pl.when(step == 0)
    def build():
        for q in range(streams):
            front_copy(0, 0, q).start()
        for g in range(groups):
            state[g] = 0
            state[groups + g] = 0
        state[2 * groups] = 0

        @pl.loop(0, tiles_ref.shape[0])
        def place_tile(t):
            @pl.when(chosen(t))
            def _():
                g = group_of(t)
                at = state[g]

                @pl.when(lax.rem(at, STACK) == 0)
                def _():
                    state[groups + g] = state[2 * groups]
                    groups_of[state[2 * groups]] = g
                    state[2 * groups] += 1

                item = state[groups + g]
                places[item, lax.rem(at, STACK)] = meta_ref[0, t]
                tile_copy(t, item, lax.rem(at, STACK)).start()
                state[g] = at + 1

        for g in range(groups):
            used = lax.rem(state[g], STACK)

            @pl.loop(used, jnp.where(used == 0, 0, STACK))
            def fill(place):
                clear(state[groups + g], place)

        items = state[2 * groups]

        @pl.loop(items, (items + STACK - 1) // STACK * STACK)
        def fill_item(item):
            groups_of[item] = 0
            for place in range(STACK):
                clear(item, place)

        @pl.loop(0, tiles_ref.shape[0])
        def wait_tile(t):
            @pl.when(chosen(t))
            def _():
                tile_copy(t, 0, 0).wait()

    @pl.when(step + 1 < pl.num_programs(0))
    def ahead():
        for q in range(streams):
            front_copy(step + 1, 1 - slot, q).start()

    for q in range(streams):
        front_copy(step, slot, q).wait()

    acc[...] = jnp.zeros_like(acc)

    @pl.loop(0, (state[2 * groups] + STACK - 1) // STACK)
    def add(s):
        products = []
        for i in range(STACK):
            item = s * STACK + i
            lefts = [pl.multiple_of(places[item, j] * TILE, TILE) for j in range(STACK)]
            rows = [held[slot, :, pl.ds(left, TILE)] for left in lefts]
            products.append(dot32(jnp.concatenate(rows, axis=1), stack[item]))
        for i in range(STACK):
            acc[groups_of[s * STACK + i]] += products[i]

    for g in range(groups):
        out, dest = outs[g // n_col], g % n_col
        if flats[g // n_col]:
            out[:, dest * TILE : (dest + 1) * TILE] = acc[g].astype(out.dtype)
        else:
            out[dest] = acc[g].astype(out.dtype)


def front_products(front, tiles, meta, subs, flats, n_col, after=()):
    rows, depth = front.shape
    groups = n_col * len(subs)
    block = largest_tile(rows, 512)
    streams = 8 if block % 128 == 0 else 1
    count = tiles.shape[0]
    items = (-(-count // STACK) + groups + STACK) // STACK * STACK
    shapes, specs = [], []
    for flat in flats:
        if flat:
            shapes.append((rows, n_col * TILE))
            specs.append(pl.BlockSpec((block, n_col * TILE), lambda i, m: (i, 0)))
        else:
            shapes.append((n_col, rows, TILE))
            specs.append(pl.BlockSpec((n_col, block, TILE), lambda i, m: (0, i, 0)))
    return pl.pallas_call(
        functools.partial(front_kernel, subs, flats, n_col, len(after)),
        grid_spec=pltpu.PrefetchScalarGridSpec(
            num_scalar_prefetch=1,
            grid=(rows // block,),
            in_specs=[in_place()] * (2 + len(after)),
            out_specs=specs,
            scratch_shapes=[
                pltpu.VMEM((items, STACK * TILE, TILE), front.dtype),
                pltpu.VMEM((2, block, depth), front.dtype),
                pltpu.VMEM((groups, block, TILE), jnp.float32),
                pltpu.SMEM((items, STACK), jnp.int32),
                pltpu.SMEM((items,), jnp.int32),
                pltpu.SMEM((2 * groups + 1,), jnp.int32),
                pltpu.SemaphoreType.DMA((count,)),
                pltpu.SemaphoreType.DMA((2, streams)),
            ],
        ),
        out_shape=[jax.ShapeDtypeStruct(shape, front.dtype) for shape in shapes],
        compiler_params=kernel_params(),
        cost_estimate=declared(),
        name="front_products",
    )(meta, tiles, front, *after)


def one_hot(want, depth, kind):
    places = lax.broadcasted_iota(jnp.int32, (want.shape[0], depth), 1)
    return (places == want).astype(jnp.float32).astype(kind)


def pack_kernel(n_row, n_solved, index_ref, *refs):
    outs = refs[-2:]
    solved = jnp.concatenate([ref[...] for ref in refs[:n_solved]], axis=1)
    cap = outs[0].shape[0] * 2 // n_row
    for k in range(n_row):
        picks = one_hot(index_ref[k * cap : (k + 1) * cap, :], solved.shape[0], solved.dtype)
        at = k // 2 * cap
        outs[k % 2][at : at + cap, :] = dot32(picks, solved).astype(outs[0].dtype)


def pack_rows(index, solved, n_row, cap, after=(), share=0):
    depth = solved[0].shape[0]
    width = sum(part.shape[1] for part in solved)
    return pl.pallas_call(
        functools.partial(pack_kernel, n_row, len(solved)),
        in_specs=[whole_block(*index.shape)]
        + [whole_block(*part.shape) for part in solved]
        + [in_place()] * len(after),
        out_shape=[jax.ShapeDtypeStruct((n_row // 2 * cap, width), solved[0].dtype)] * 2,
        compiler_params=kernel_params(),
        cost_estimate=declared(share * n_row * cap * depth * width),
        name="pack_rows",
    )(index, *solved, *after)


def join_pieces(pieces, joined):
    at = 0
    for piece in pieces:
        joined[at : at + piece.shape[0], :] = piece[...]
        at += piece.shape[0]


def assemble_kernel(n_pieces, index_ref, bem_ref, *refs):
    outs, joined = refs[-3:-1], refs[-1]
    join_pieces(refs[:n_pieces], joined)
    count = outs[0].shape[0]
    step = largest_tile(count, 512)
    for half, out in enumerate(outs):
        for i in range(0, count, step):
            want = index_ref[half * count + i : half * count + i + step, :]
            taken = dot32(one_hot(want, joined.shape[0], joined.dtype), joined[...])
            entries = bem_ref[half, i : i + step, :].astype(jnp.float32)
            out[i : i + step, :] = (entries - taken).astype(out.dtype)


def assemble(index, bem, pieces, start, after=()):
    width = pieces[0].shape[1]
    routed = sum(piece.shape[0] for piece in pieces)
    count = bem.shape[1]
    place = start * TILE // width
    return pl.pallas_call(
        functools.partial(assemble_kernel, len(pieces)),
        grid=(1,),
        in_specs=[
            whole_block(*index.shape),
            pl.BlockSpec((2, count, width), lambda i: (0, 0, place)),
        ]
        + [whole_block(*piece.shape) for piece in pieces]
        + [in_place()] * len(after),
        out_specs=[whole_block(count, width)] * 2,
        out_shape=[jax.ShapeDtypeStruct((count, width), bem.dtype)] * 2,
        scratch_shapes=[pltpu.VMEM((routed, width), bem.dtype)],
        compiler_params=kernel_params(),
        cost_estimate=declared(4 * 2 * count * routed * width),
        name="assemble",
    )(index, bem, *pieces, *after)


def subtract_kernel(bem_ref, schur_ref, *refs):
    taken = schur_ref[...].astype(jnp.float32)
    refs[-1][...] = (bem_ref[...].astype(jnp.float32) - taken).astype(refs[-1].dtype)


def subtract(bem, schur, first, start, after=()):
    halves, count, width = schur.shape
    place = start * TILE // width
    return pl.pallas_call(
        subtract_kernel,
        grid=(1,),
        in_specs=[
            pl.BlockSpec((halves, count, width), lambda i: (first, 0, place)),
            whole_block(halves, count, width),
        ]
        + [in_place()] * len(after),
        out_specs=whole_block(halves, count, width),
        out_shape=jax.ShapeDtypeStruct((halves, count, width), bem.dtype),
        compiler_params=kernel_params(),
        cost_estimate=declared(),
        name="subtract",
    )(bem, schur, *after)


def unpack_kernel(n_pieces, n_col, parts, index_ref, *refs):
    outs, joined = refs[-1 - parts : -1], refs[-1]
    join_pieces(refs[:n_pieces], joined)
    _, count, width = outs[0].shape
    step = largest_tile(count, 512)
    for p, out in enumerate(outs):
        for i in range(0, count, step):
            want = index_ref[p * count + i : p * count + i + step, :]
            taken = dot32(one_hot(want, joined.shape[0], joined.dtype), joined[...])
            for d in range(n_col):
                out[d, i : i + step, :] = taken[:, d * width : (d + 1) * width].astype(out.dtype)


def unpack(index, pieces, n_col, parts, after=(), share=0):
    wide = pieces[0].shape[1]
    routed = sum(piece.shape[0] for piece in pieces)
    count, width = index.shape[0] // parts, wide // n_col
    return pl.pallas_call(
        functools.partial(unpack_kernel, len(pieces), n_col, parts),
        in_specs=[whole_block(*index.shape)]
        + [whole_block(*piece.shape) for piece in pieces]
        + [in_place()] * len(after),
        out_shape=[jax.ShapeDtypeStruct((n_col, count, width), pieces[0].dtype)] * parts,
        scratch_shapes=[pltpu.VMEM((routed, wide), pieces[0].dtype)],
        compiler_params=kernel_params(),
        cost_estimate=declared(share * parts * count * routed * wide),
        name="unpack",
    )(index, *pieces, *after)


def product_kernel(streams, minus, order_ref, *refs):
    blocks, (near_ref, far_ref) = refs[:streams], refs[streams : streams + 2]
    out_ref, acc = refs[-2:]
    k = pl.program_id(0)
    steps = pl.num_programs(0)
    half = steps // 2
    deep = near_ref.shape[0] // half

    def term(rows_ref, at):
        matrix = jnp.concatenate([block[...] for block in blocks], axis=1)
        return dot32(matrix, rows_ref[pl.ds(pl.multiple_of(at * deep, deep), deep), :])

    @pl.when(k == 0)
    def _():
        acc[...] = term(near_ref, 0)

    @pl.when((k > 0) & (k < half))
    def _():
        acc[...] += term(near_ref, k)

    @pl.when(k >= half)
    def _():
        acc[...] += term(far_ref, k - half)

    @pl.when(k == steps - 1)
    def _():
        total = acc[...]
        if minus:
            total = refs[streams + 2][...].astype(jnp.float32) - total
        out_ref[...] = total.astype(out_ref.dtype)


def product(matrix, order, near, far, base=None, after=()):
    rows, depth = matrix.shape
    width = near.shape[1]
    n_row = order.shape[0]
    deep = depth // n_row
    streams = 4 if deep % (4 * TILE) == 0 else 1
    bases = [] if base is None else [base]

    def block_of(q):
        return pl.BlockSpec((rows, deep // streams), lambda k, order: (0, order[k] * streams + q))

    return pl.pallas_call(
        functools.partial(product_kernel, streams, bool(bases)),
        grid_spec=pltpu.PrefetchScalarGridSpec(
            num_scalar_prefetch=1,
            grid=(n_row,),
            in_specs=[block_of(q) for q in range(streams)]
            + [whole_block(*near.shape)] * 2
            + [whole_block(rows, width)] * len(bases)
            + [in_place()] * len(after),
            out_specs=whole_block(rows, width),
            scratch_shapes=[pltpu.VMEM((rows, width), jnp.float32)],
        ),
        out_shape=jax.ShapeDtypeStruct((rows, width), near.dtype),
        compiler_params=kernel_params(),
        cost_estimate=declared(6 * rows * depth * max(width, 256)),
        name="product",
    )(order, *[matrix] * streams, near, far, *bases, *after)


def exchange(value, distance, n, axis="row"):
    return lax.ppermute(value, axis, [(i, i ^ distance) for i in range(n)])


def route(packed, n_row):
    near, far = packed[0], exchange(packed[1], 1, n_row)
    cap = near.shape[0] * 2 // n_row
    sent = []
    for i in range(1, n_row // 2):
        both = [near[i * cap : (i + 1) * cap], far[i * cap : (i + 1) * cap]]
        sent.append(jnp.concatenate(both, axis=0))
    pieces = [exchange(both, 2 * i, n_row) for i, both in enumerate(sent, 1)]
    return [near[:cap], far[:cap]] + pieces, tuple(sent)


def gather_rows(block, n_row):
    near = [block] + [exchange(block, k, n_row) for k in range(2, n_row, 2)]
    near = jnp.concatenate(near, axis=0)
    return near, exchange(near, 1, n_row)


def route_tables(surface_map, rows, n_row, cap, slots):
    me = lax.axis_index("row")
    mine = surface_map.reshape(-1)
    every = lax.all_gather(mine, "row")
    partners = me ^ jnp.arange(n_row, dtype=jnp.int32)
    local = every[partners] - me * rows
    asked = (local >= 0) & (local < rows)
    rank = jnp.cumsum(asked.astype(jnp.int32), axis=1) - 1
    numbers = jnp.arange(slots, dtype=jnp.int32)
    hit = asked[:, None, :] & (rank[:, None, :] == numbers[None, :, None])
    wanted = jnp.sum(jnp.where(hit, local[:, None, :] + 1, 0), axis=2) - 1
    owner = mine // rows
    held = owner[None, :] == jnp.arange(n_row, dtype=jnp.int32)[:, None]
    place = jnp.cumsum(held.astype(jnp.int32), axis=1) - 1
    slot = jnp.sum(jnp.where(held, place, 0), axis=0)
    lands = (owner ^ me) * slots + slot
    return wanted.reshape(-1, 1), lands.reshape(-1, 1)


def per_device(
    front_inverse,
    coupling_tiles,
    tile_row,
    tile_col,
    surface_map,
    bem_entries,
    pivot_inverse,
    slab_below,
):
    n_row, n_col = lax.axis_size("row"), lax.axis_size("col")
    assert n_row > 1 and n_row & (n_row - 1) == 0
    rows, depth = front_inverse.shape
    count = bem_entries.shape[1]
    per_dest = bem_entries.shape[2] // TILE
    cap = rows // n_row
    slots = -(-cap // 16) * 16
    me = lax.axis_index("row")

    col_at = lax.axis_index("col")
    block_row = tile_row - col_at * (depth // TILE)
    dest, sub = tile_col // per_dest, tile_col % per_dest
    meta = jnp.stack([block_row, dest, sub])
    order = me ^ jnp.concatenate(
        [jnp.arange(0, n_row, 2, dtype=jnp.int32), jnp.arange(1, n_row, 2, dtype=jnp.int32)]
    )
    half = per_dest // 2
    assert per_dest == 2 * half

    def summed(parts):
        return lax.psum_scatter(parts, "col", scatter_dimension=0)

    solved, uppers, lowers = [], [], []

    def unpack_next(after, share):
        upper, lower = unpack(lands, pieces, n_col, 2, after, share)
        uppers.append(summed(upper).reshape(1, count, TILE))
        lowers.append(lower)
        return upper

    sent = ()
    for sub in range(half):
        parts, flat = front_products(
            front_inverse, coupling_tiles, meta, (sub, half + sub), (False, True), n_col, sent
        )
        solved.append(summed(parts))
        if sub == 0:
            wanted, lands = route_tables(surface_map, rows, n_row, cap, slots)
            after = ()
        else:
            after = (unpack_next((flat,), 0),)
        packed = pack_rows(wanted, [flat], n_row, slots, after, 4 if sub else 0)
        pieces, sent = route(packed, n_row)
    packed = pack_rows(wanted, solved, n_row, slots, (packed[0],), 4)
    upper = unpack_next((packed[0],), 4)
    lowers = [summed(low).reshape(1, count, TILE) for low in lowers]

    last, base = assemble(lands, bem_entries, route(packed, n_row)[0], 0, (upper,))
    gathered = [gather_rows(last, n_row)]
    for at, schur in enumerate(uppers):
        last = subtract(bem_entries, schur, 0, half + at, (last,))[0]
        gathered.append(gather_rows(last, n_row))
    pivots, belows = [], []
    for near, far in gathered:
        last = product(pivot_inverse, order, near, far, after=(last,))
        pivots.append(last)
    gathered = [gather_rows(pivot, n_row) for pivot in pivots]
    for g, (near, far) in enumerate(gathered):
        if g > 0:
            base = subtract(bem_entries, lowers[g - 1], 1, half + g - 1, (last,))[0]
        last = product(slab_below, order, near, far, base, (last,))
        belows.append(last)
    return jnp.stack([jnp.concatenate(parts, axis=1) for parts in (pivots, belows)])


def solution(mesh):
    placed = (
        P("row", "col"),
        P("col", None, None),
        P("col"),
        P("col"),
        P(None, "row"),
        P(None, "row", "col"),
        P("row", None),
        P("row", None),
    )
    return jax.shard_map(
        per_device, mesh=mesh, in_specs=placed, out_specs=P(None, "row", "col"), check_vma=False
    )
```

```python
import functools

import jax
import jax.numpy as jnp
from jax import lax
from jax.experimental import pallas as pl
from jax.experimental.pallas import tpu as pltpu
from jax.sharding import PartitionSpec as P

TILE = 128
STACK = 4
VMEM_BYTES = 56 * 1024 * 1024


def largest_tile(total, most):
    best = total
    for size in range(16, most + 1, 16):
        if total % size == 0:
            best = size
    return best


def kernel_params():
    return pltpu.CompilerParams(vmem_limit_bytes=VMEM_BYTES)


def declared(flops=0):
    return pl.CostEstimate(flops=flops, bytes_accessed=1, transcendentals=0)


def whole_block(*shape):
    return pl.BlockSpec(shape, lambda *_: (0,) * len(shape))


def in_place():
    return pl.BlockSpec(memory_space=pl.ANY)


def dot32(left, right):
    return jnp.dot(left, right, preferred_element_type=jnp.float32)


def front_kernel(subs, flats, n_col, n_after, meta_ref, tiles_ref, front_ref, *refs):
    outs = refs[n_after : n_after + len(subs)]
    stack, held, acc, places, groups_of, state, tile_sems, sems = refs[n_after + len(subs) :]
    groups = n_col * len(subs)
    block, streams = held.shape[1], sems.shape[1]
    lines = block // streams
    step = pl.program_id(0)
    slot = lax.rem(step, 2)

    def front_copy(at, into, q):
        return pltpu.make_async_copy(
            front_ref.at[pl.ds(pl.multiple_of(at * block + q * lines, lines), lines), :],
            held.at[into, pl.ds(q * lines, lines), :],
            sems.at[into, q],
        )

    def tile_copy(t, item, place):
        return pltpu.make_async_copy(
            tiles_ref.at[t],
            stack.at[item, pl.ds(pl.multiple_of(place * TILE, TILE), TILE), :],
            tile_sems.at[t],
        )

    def chosen(t):
        return functools.reduce(jnp.logical_or, [meta_ref[2, t] == sub for sub in subs])

    def group_of(t):
        order = 0
        for p in range(1, len(subs)):
            order = jnp.where(meta_ref[2, t] == subs[p], p, order)
        return order * n_col + meta_ref[1, t]

    def clear(item, place):
        places[item, place] = 0
        stack[item, pl.ds(pl.multiple_of(place * TILE, TILE), TILE), :] = jnp.zeros(
            (TILE, TILE), stack.dtype
        )

    @pl.when(step == 0)
    def build():
        for q in range(streams):
            front_copy(0, 0, q).start()
        for g in range(groups):
            state[g] = 0
            state[groups + g] = 0
        state[2 * groups] = 0

        @pl.loop(0, tiles_ref.shape[0])
        def place_tile(t):
            @pl.when(chosen(t))
            def _():
                g = group_of(t)
                at = state[g]

                @pl.when(lax.rem(at, STACK) == 0)
                def _():
                    state[groups + g] = state[2 * groups]
                    groups_of[state[2 * groups]] = g
                    state[2 * groups] += 1

                item = state[groups + g]
                places[item, lax.rem(at, STACK)] = meta_ref[0, t]
                tile_copy(t, item, lax.rem(at, STACK)).start()
                state[g] = at + 1

        for g in range(groups):
            used = lax.rem(state[g], STACK)

            @pl.loop(used, jnp.where(used == 0, 0, STACK))
            def fill(place):
                clear(state[groups + g], place)

        items = state[2 * groups]

        @pl.loop(items, (items + STACK - 1) // STACK * STACK)
        def fill_item(item):
            groups_of[item] = 0
            for place in range(STACK):
                clear(item, place)

        @pl.loop(0, tiles_ref.shape[0])
        def wait_tile(t):
            @pl.when(chosen(t))
            def _():
                tile_copy(t, 0, 0).wait()

    @pl.when(step + 1 < pl.num_programs(0))
    def ahead():
        for q in range(streams):
            front_copy(step + 1, 1 - slot, q).start()

    for q in range(streams):
        front_copy(step, slot, q).wait()

    acc[...] = jnp.zeros_like(acc)

    @pl.loop(0, (state[2 * groups] + STACK - 1) // STACK)
    def add(s):
        for i in range(STACK):
            item = s * STACK + i
            lefts = [pl.multiple_of(places[item, j] * TILE, TILE) for j in range(STACK)]
            rows = [held[slot, :, pl.ds(left, TILE)] for left in lefts]
            acc[groups_of[item]] += dot32(jnp.concatenate(rows, axis=1), stack[item])

    for g in range(groups):
        out, dest = outs[g // n_col], g % n_col
        if flats[g // n_col]:
            out[:, dest * TILE : (dest + 1) * TILE] = acc[g].astype(out.dtype)
        else:
            out[dest] = acc[g].astype(out.dtype)


def front_products(front, tiles, meta, subs, flats, n_col, after=()):
    rows, depth = front.shape
    groups = n_col * len(subs)
    block = largest_tile(rows, 512)
    streams = 8 if block % 128 == 0 else 1
    count = tiles.shape[0]
    items = (-(-count // STACK) + groups + STACK) // STACK * STACK
    shapes, specs = [], []
    for flat in flats:
        if flat:
            shapes.append((rows, n_col * TILE))
            specs.append(pl.BlockSpec((block, n_col * TILE), lambda i, m: (i, 0)))
        else:
            shapes.append((n_col, rows, TILE))
            specs.append(pl.BlockSpec((n_col, block, TILE), lambda i, m: (0, i, 0)))
    return pl.pallas_call(
        functools.partial(front_kernel, subs, flats, n_col, len(after)),
        grid_spec=pltpu.PrefetchScalarGridSpec(
            num_scalar_prefetch=1,
            grid=(rows // block,),
            in_specs=[in_place()] * (2 + len(after)),
            out_specs=specs,
            scratch_shapes=[
                pltpu.VMEM((items, STACK * TILE, TILE), front.dtype),
                pltpu.VMEM((2, block, depth), front.dtype),
                pltpu.VMEM((groups, block, TILE), jnp.float32),
                pltpu.SMEM((items, STACK), jnp.int32),
                pltpu.SMEM((items,), jnp.int32),
                pltpu.SMEM((2 * groups + 1,), jnp.int32),
                pltpu.SemaphoreType.DMA((count,)),
                pltpu.SemaphoreType.DMA((2, streams)),
            ],
        ),
        out_shape=[jax.ShapeDtypeStruct(shape, front.dtype) for shape in shapes],
        compiler_params=kernel_params(),
        cost_estimate=declared(),
        name="front_products",
    )(meta, tiles, front, *after)


def one_hot(want, depth, kind):
    places = lax.broadcasted_iota(jnp.int32, (want.shape[0], depth), 1)
    return (places == want).astype(jnp.float32).astype(kind)


def pack_kernel(n_row, n_solved, index_ref, *refs):
    outs = refs[-2:]
    solved = jnp.concatenate([ref[...] for ref in refs[:n_solved]], axis=1)
    cap = outs[0].shape[0] * 2 // n_row
    for k in range(n_row):
        picks = one_hot(index_ref[k * cap : (k + 1) * cap, :], solved.shape[0], solved.dtype)
        at = k // 2 * cap
        outs[k % 2][at : at + cap, :] = dot32(picks, solved).astype(outs[0].dtype)


def pack_rows(index, solved, n_row, cap, after=(), share=0):
    depth = solved[0].shape[0]
    width = sum(part.shape[1] for part in solved)
    return pl.pallas_call(
        functools.partial(pack_kernel, n_row, len(solved)),
        in_specs=[whole_block(*index.shape)]
        + [whole_block(*part.shape) for part in solved]
        + [in_place()] * len(after),
        out_shape=[jax.ShapeDtypeStruct((n_row // 2 * cap, width), solved[0].dtype)] * 2,
        compiler_params=kernel_params(),
        cost_estimate=declared(share * n_row * cap * depth * width),
        name="pack_rows",
    )(index, *solved, *after)


def join_pieces(pieces, joined):
    at = 0
    for piece in pieces:
        joined[at : at + piece.shape[0], :] = piece[...]
        at += piece.shape[0]


def assemble_kernel(n_pieces, index_ref, bem_ref, *refs):
    outs, joined = refs[-3:-1], refs[-1]
    join_pieces(refs[:n_pieces], joined)
    count = outs[0].shape[0]
    step = largest_tile(count, 512)
    for half, out in enumerate(outs):
        for i in range(0, count, step):
            want = index_ref[half * count + i : half * count + i + step, :]
            taken = dot32(one_hot(want, joined.shape[0], joined.dtype), joined[...])
            entries = bem_ref[half, i : i + step, :].astype(jnp.float32)
            out[i : i + step, :] = (entries - taken).astype(out.dtype)


def assemble(index, bem, pieces, start, after=()):
    width = pieces[0].shape[1]
    routed = sum(piece.shape[0] for piece in pieces)
    count = bem.shape[1]
    place = start * TILE // width
    return pl.pallas_call(
        functools.partial(assemble_kernel, len(pieces)),
        grid=(1,),
        in_specs=[
            whole_block(*index.shape),
            pl.BlockSpec((2, count, width), lambda i: (0, 0, place)),
        ]
        + [whole_block(*piece.shape) for piece in pieces]
        + [in_place()] * len(after),
        out_specs=[whole_block(count, width)] * 2,
        out_shape=[jax.ShapeDtypeStruct((count, width), bem.dtype)] * 2,
        scratch_shapes=[pltpu.VMEM((routed, width), bem.dtype)],
        compiler_params=kernel_params(),
        cost_estimate=declared(4 * 2 * count * routed * width),
        name="assemble",
    )(index, bem, *pieces, *after)


def subtract_kernel(n_parts, bem_ref, *refs):
    out = refs[-1]
    for at, part in enumerate(refs[:n_parts]):
        columns = slice(at * TILE, (at + 1) * TILE)
        taken = part[...].astype(jnp.float32)
        out[:, columns] = (bem_ref[0, :, columns].astype(jnp.float32) - taken).astype(out.dtype)


def subtract(bem, parts, half, start, after=()):
    count, width = bem.shape[1], len(parts) * TILE
    place = start * TILE // width

    def rows_of(part):
        at = half if part.shape[0] > count else 0
        return pl.BlockSpec((count, TILE), lambda i: (at, 0))

    return pl.pallas_call(
        functools.partial(subtract_kernel, len(parts)),
        grid=(1,),
        in_specs=[pl.BlockSpec((1, count, width), lambda i: (half, 0, place))]
        + [rows_of(part) for part in parts]
        + [in_place()] * len(after),
        out_specs=whole_block(count, width),
        out_shape=jax.ShapeDtypeStruct((count, width), bem.dtype),
        compiler_params=kernel_params(),
        cost_estimate=declared(),
        name="subtract",
    )(bem, *parts, *after)


def join_kernel(n_parts, *refs):
    join_pieces(refs[:n_parts], refs[-1])


def join(parts, after=()):
    depth, width = sum(part.shape[0] for part in parts), parts[0].shape[1]
    return pl.pallas_call(
        functools.partial(join_kernel, len(parts)),
        in_specs=[whole_block(*part.shape) for part in parts] + [in_place()] * len(after),
        out_shape=jax.ShapeDtypeStruct((depth, width), parts[0].dtype),
        compiler_params=kernel_params(),
        cost_estimate=declared(),
        name="join",
    )(*parts, *after)


def unpack_kernel(n_pieces, n_col, parts, index_ref, *refs):
    outs, joined = refs[-1 - parts : -1], refs[-1]
    join_pieces(refs[:n_pieces], joined)
    _, count, width = outs[0].shape
    step = largest_tile(count, 512)
    for p, out in enumerate(outs):
        for i in range(0, count, step):
            want = index_ref[p * count + i : p * count + i + step, :]
            taken = dot32(one_hot(want, joined.shape[0], joined.dtype), joined[...])
            for d in range(n_col):
                out[d, i : i + step, :] = taken[:, d * width : (d + 1) * width].astype(out.dtype)


def unpack(index, pieces, n_col, parts, after=(), share=0):
    wide = pieces[0].shape[1]
    routed = sum(piece.shape[0] for piece in pieces)
    count, width = index.shape[0] // parts, wide // n_col
    return pl.pallas_call(
        functools.partial(unpack_kernel, len(pieces), n_col, parts),
        in_specs=[whole_block(*index.shape)]
        + [whole_block(*piece.shape) for piece in pieces]
        + [in_place()] * len(after),
        out_shape=[jax.ShapeDtypeStruct((n_col, count, width), pieces[0].dtype)] * parts,
        scratch_shapes=[pltpu.VMEM((routed, wide), pieces[0].dtype)],
        compiler_params=kernel_params(),
        cost_estimate=declared(share * parts * count * routed * wide),
        name="unpack",
    )(index, *pieces, *after)


def product_kernel(streams, minus, order_ref, *refs):
    blocks, (near_ref, far_ref) = refs[:streams], refs[streams : streams + 2]
    out_ref, acc = refs[-2:]
    k = pl.program_id(0)
    steps = pl.num_programs(0)
    half = steps // 2
    deep = near_ref.shape[0] // half

    def term(rows_ref, at):
        matrix = jnp.concatenate([block[...] for block in blocks], axis=1)
        return dot32(matrix, rows_ref[pl.ds(pl.multiple_of(at * deep, deep), deep), :])

    @pl.when(k == 0)
    def _():
        acc[...] = term(near_ref, 0)

    @pl.when((k > 0) & (k < half))
    def _():
        acc[...] += term(near_ref, k)

    @pl.when(k >= half)
    def _():
        acc[...] += term(far_ref, k - half)

    @pl.when(k == steps - 1)
    def _():
        total = acc[...]
        if minus:
            total = refs[streams + 2][...].astype(jnp.float32) - total
        out_ref[...] = total.astype(out_ref.dtype)


def product(matrix, order, near, far, base=None, after=()):
    rows, depth = matrix.shape
    width = near.shape[1]
    n_row = order.shape[0]
    deep = depth // n_row
    streams = 4 if deep % (4 * TILE) == 0 else 1
    bases = [] if base is None else [base]

    def block_of(q):
        return pl.BlockSpec((rows, deep // streams), lambda k, order: (0, order[k] * streams + q))

    return pl.pallas_call(
        functools.partial(product_kernel, streams, bool(bases)),
        grid_spec=pltpu.PrefetchScalarGridSpec(
            num_scalar_prefetch=1,
            grid=(n_row,),
            in_specs=[block_of(q) for q in range(streams)]
            + [whole_block(*near.shape)] * 2
            + [whole_block(rows, width)] * len(bases)
            + [in_place()] * len(after),
            out_specs=whole_block(rows, width),
            scratch_shapes=[pltpu.VMEM((rows, width), jnp.float32)],
        ),
        out_shape=jax.ShapeDtypeStruct((rows, width), near.dtype),
        compiler_params=kernel_params(),
        cost_estimate=declared(6 * rows * depth * max(width, 256)),
        name="product",
    )(order, *[matrix] * streams, near, far, *bases, *after)


def exchange(value, distance, n, axis="row"):
    return lax.ppermute(value, axis, [(i, i ^ distance) for i in range(n)])


def route(packed, n_row):
    near, far = packed[0], exchange(packed[1], 1, n_row)
    cap = near.shape[0] * 2 // n_row
    sent = []
    for i in range(1, n_row // 2):
        both = [near[i * cap : (i + 1) * cap], far[i * cap : (i + 1) * cap]]
        sent.append(jnp.concatenate(both, axis=0))
    pieces = [exchange(both, 2 * i, n_row) for i, both in enumerate(sent, 1)]
    return [near[:cap], far[:cap]] + pieces, tuple(sent)


def gather_rows(block, n_row):
    return [block] + [exchange(block, k, n_row) for k in range(2, n_row, 2)]


def both_cores(near, n_row):
    return near, exchange(near, 1, n_row)


def route_tables(surface_map, rows, n_row, cap, slots):
    me = lax.axis_index("row")
    mine = surface_map.reshape(-1)
    every = lax.all_gather(mine, "row")
    partners = me ^ jnp.arange(n_row, dtype=jnp.int32)
    local = every[partners] - me * rows
    asked = (local >= 0) & (local < rows)
    rank = jnp.cumsum(asked.astype(jnp.int32), axis=1) - 1
    numbers = jnp.arange(slots, dtype=jnp.int32)
    hit = asked[:, None, :] & (rank[:, None, :] == numbers[None, :, None])
    wanted = jnp.sum(jnp.where(hit, local[:, None, :] + 1, 0), axis=2) - 1
    owner = mine // rows
    held = owner[None, :] == jnp.arange(n_row, dtype=jnp.int32)[:, None]
    place = jnp.cumsum(held.astype(jnp.int32), axis=1) - 1
    slot = jnp.sum(jnp.where(held, place, 0), axis=0)
    lands = (owner ^ me) * slots + slot
    return wanted.reshape(-1, 1), lands.reshape(-1, 1)


def per_device(
    front_inverse,
    coupling_tiles,
    tile_row,
    tile_col,
    surface_map,
    bem_entries,
    pivot_inverse,
    slab_below,
):
    n_row, n_col = lax.axis_size("row"), lax.axis_size("col")
    assert n_row > 1 and n_row & (n_row - 1) == 0
    rows, depth = front_inverse.shape
    count = bem_entries.shape[1]
    per_dest = bem_entries.shape[2] // TILE
    cap = rows // n_row
    slots = -(-cap // 16) * 16
    me = lax.axis_index("row")

    col_at = lax.axis_index("col")
    block_row = tile_row - col_at * (depth // TILE)
    dest, sub = tile_col // per_dest, tile_col % per_dest
    meta = jnp.stack([block_row, dest, sub])
    order = me ^ jnp.concatenate(
        [jnp.arange(0, n_row, 2, dtype=jnp.int32), jnp.arange(1, n_row, 2, dtype=jnp.int32)]
    )
    half = per_dest // 2
    assert per_dest == 2 * half

    def summed(parts):
        return lax.psum_scatter(parts, "col", scatter_dimension=0)

    parts = front_products(
        front_inverse, coupling_tiles, meta, tuple(range(half)), (False,) * half, n_col
    )
    solved = [summed(part) for part in parts]
    flats = front_products(
        front_inverse, coupling_tiles, meta, tuple(range(half, per_dest)), (True,) * half, n_col,
        (parts[0],),
    )
    wanted, lands = route_tables(surface_map, rows, n_row, cap, slots)
    routed, after = [], ()
    for flat in flats:
        packed = pack_rows(wanted, [flat], n_row, slots, after)
        pieces, after = route(packed, n_row)
        routed.append(pieces)
    after = (packed[0],)

    uppers, lowers = [], []
    for at, pieces in enumerate(routed):
        cuts = unpack(lands, pieces, n_col, 1 if at + 1 < half else 2, after, 12)
        uppers.append(summed(cuts[0]))
        lowers.append(cuts[1:])
        after = (cuts[0],)
        if at == 0:
            packed = pack_rows(wanted, solved, n_row, slots, after, 12)
            after = (packed[0],)
    lowers = [summed(low[0]) if low else both for low, both in zip(lowers, uppers)]

    upper, lower = assemble(lands, bem_entries, route(packed, n_row)[0], 0, after)
    first = gather_rows(upper, n_row)
    upper = subtract(bem_entries, uppers, 0, half, (upper,))
    second = gather_rows(upper, n_row)
    near, far = both_cores(join(first, (upper,)), n_row)
    pivots = [product(pivot_inverse, order, near, far, after=(upper,))]
    first = gather_rows(pivots[0], n_row)
    near, far = both_cores(join(second, (pivots[0],)), n_row)
    pivots.append(product(pivot_inverse, order, near, far, after=(pivots[0],)))
    second = gather_rows(pivots[1], n_row)
    near, far = both_cores(join(first, (pivots[1],)), n_row)
    below = subtract(bem_entries, lowers, 1, half, (pivots[1],))
    belows = [product(slab_below, order, near, far, lower, (below,))]
    near, far = both_cores(join(second, (belows[0],)), n_row)
    belows.append(product(slab_below, order, near, far, below))
    return jnp.stack([jnp.concatenate(parts, axis=1) for parts in (pivots, belows)])


def solution(mesh):
    placed = (
        P("row", "col"),
        P("col", None, None),
        P("col"),
        P("col"),
        P(None, "row"),
        P(None, "row", "col"),
        P("row", None),
        P("row", None),
    )
    return jax.shard_map(
        per_device, mesh=mesh, in_specs=placed, out_specs=P(None, "row", "col"), check_vma=False
    )
```

```python
import functools

import jax
import jax.numpy as jnp
from jax import lax
from jax.experimental import pallas as pl
from jax.experimental.pallas import tpu as pltpu
from jax.sharding import PartitionSpec as P

TILE = 128
STACK = 4
VMEM_BYTES = 56 * 1024 * 1024


def largest_tile(total, most):
    best = total
    for size in range(16, most + 1, 16):
        if total % size == 0:
            best = size
    return best


def kernel_params():
    return pltpu.CompilerParams(vmem_limit_bytes=VMEM_BYTES)


def declared(flops=0):
    return pl.CostEstimate(flops=flops, bytes_accessed=1, transcendentals=0)


def whole_block(*shape):
    return pl.BlockSpec(shape, lambda *_: (0,) * len(shape))


def in_place():
    return pl.BlockSpec(memory_space=pl.ANY)


def dot32(left, right):
    return jnp.dot(left, right, preferred_element_type=jnp.float32)


def front_kernel(subs, flats, n_col, n_after, meta_ref, tiles_ref, front_ref, *refs):
    outs = refs[n_after : n_after + len(subs)]
    stack, held, acc, places, groups_of, state, tile_sems, sems = refs[n_after + len(subs) :]
    groups = n_col * len(subs)
    block, streams = held.shape[1], sems.shape[1]
    lines = block // streams
    step = pl.program_id(0)
    slot = lax.rem(step, 2)

    def front_copy(at, into, q):
        return pltpu.make_async_copy(
            front_ref.at[pl.ds(pl.multiple_of(at * block + q * lines, lines), lines), :],
            held.at[into, pl.ds(q * lines, lines), :],
            sems.at[into, q],
        )

    def tile_copy(t, item, place):
        return pltpu.make_async_copy(
            tiles_ref.at[t],
            stack.at[item, pl.ds(pl.multiple_of(place * TILE, TILE), TILE), :],
            tile_sems.at[t],
        )

    def chosen(t):
        return functools.reduce(jnp.logical_or, [meta_ref[2, t] == sub for sub in subs])

    def group_of(t):
        order = 0
        for p in range(1, len(subs)):
            order = jnp.where(meta_ref[2, t] == subs[p], p, order)
        return order * n_col + meta_ref[1, t]

    def clear(item, place):
        places[item, place] = 0
        stack[item, pl.ds(pl.multiple_of(place * TILE, TILE), TILE), :] = jnp.zeros(
            (TILE, TILE), stack.dtype
        )

    @pl.when(step == 0)
    def build():
        for q in range(streams):
            front_copy(0, 0, q).start()
        for g in range(groups):
            state[g] = 0
            state[groups + g] = 0
        state[2 * groups] = 0

        @pl.loop(0, tiles_ref.shape[0])
        def place_tile(t):
            @pl.when(chosen(t))
            def _():
                g = group_of(t)
                at = state[g]

                @pl.when(lax.rem(at, STACK) == 0)
                def _():
                    state[groups + g] = state[2 * groups]
                    groups_of[state[2 * groups]] = g
                    state[2 * groups] += 1

                item = state[groups + g]
                places[item, lax.rem(at, STACK)] = meta_ref[0, t]
                tile_copy(t, item, lax.rem(at, STACK)).start()
                state[g] = at + 1

        for g in range(groups):
            used = lax.rem(state[g], STACK)

            @pl.loop(used, jnp.where(used == 0, 0, STACK))
            def fill(place):
                clear(state[groups + g], place)

        items = state[2 * groups]

        @pl.loop(items, (items + STACK - 1) // STACK * STACK)
        def fill_item(item):
            groups_of[item] = 0
            for place in range(STACK):
                clear(item, place)

        @pl.loop(0, tiles_ref.shape[0])
        def wait_tile(t):
            @pl.when(chosen(t))
            def _():
                tile_copy(t, 0, 0).wait()

    @pl.when(step + 1 < pl.num_programs(0))
    def ahead():
        for q in range(streams):
            front_copy(step + 1, 1 - slot, q).start()

    for q in range(streams):
        front_copy(step, slot, q).wait()

    acc[...] = jnp.zeros_like(acc)

    @pl.loop(0, (state[2 * groups] + STACK - 1) // STACK)
    def add(s):
        for i in range(STACK):
            item = s * STACK + i
            lefts = [pl.multiple_of(places[item, j] * TILE, TILE) for j in range(STACK)]
            rows = [held[slot, :, pl.ds(left, TILE)] for left in lefts]
            acc[groups_of[item]] += dot32(jnp.concatenate(rows, axis=1), stack[item])

    for g in range(groups):
        out, dest = outs[g // n_col], g % n_col
        if flats[g // n_col]:
            out[:, dest * TILE : (dest + 1) * TILE] = acc[g].astype(out.dtype)
        else:
            out[dest] = acc[g].astype(out.dtype)


def front_products(front, tiles, meta, subs, flats, n_col, after=()):
    rows, depth = front.shape
    groups = n_col * len(subs)
    block = largest_tile(rows, 512)
    streams = 8 if block % 128 == 0 else 1
    count = tiles.shape[0]
    items = (-(-count // STACK) + groups + STACK) // STACK * STACK
    shapes, specs = [], []
    for flat in flats:
        if flat:
            shapes.append((rows, n_col * TILE))
            specs.append(pl.BlockSpec((block, n_col * TILE), lambda i, m: (i, 0)))
        else:
            shapes.append((n_col, rows, TILE))
            specs.append(pl.BlockSpec((n_col, block, TILE), lambda i, m: (0, i, 0)))
    return pl.pallas_call(
        functools.partial(front_kernel, subs, flats, n_col, len(after)),
        grid_spec=pltpu.PrefetchScalarGridSpec(
            num_scalar_prefetch=1,
            grid=(rows // block,),
            in_specs=[in_place()] * (2 + len(after)),
            out_specs=specs,
            scratch_shapes=[
                pltpu.VMEM((items, STACK * TILE, TILE), front.dtype),
                pltpu.VMEM((2, block, depth), front.dtype),
                pltpu.VMEM((groups, block, TILE), jnp.float32),
                pltpu.SMEM((items, STACK), jnp.int32),
                pltpu.SMEM((items,), jnp.int32),
                pltpu.SMEM((2 * groups + 1,), jnp.int32),
                pltpu.SemaphoreType.DMA((count,)),
                pltpu.SemaphoreType.DMA((2, streams)),
            ],
        ),
        out_shape=[jax.ShapeDtypeStruct(shape, front.dtype) for shape in shapes],
        compiler_params=kernel_params(),
        cost_estimate=declared(),
        name="front_products",
    )(meta, tiles, front, *after)


def one_hot(want, depth, kind):
    places = lax.broadcasted_iota(jnp.int32, (want.shape[0], depth), 1)
    return (places == want).astype(jnp.float32).astype(kind)


def pack_kernel(n_row, n_solved, index_ref, *refs):
    outs = refs[-2:]
    solved = jnp.concatenate([ref[...] for ref in refs[:n_solved]], axis=1)
    cap = outs[0].shape[0] * 2 // n_row
    for k in range(n_row):
        picks = one_hot(index_ref[k * cap : (k + 1) * cap, :], solved.shape[0], solved.dtype)
        at = k // 2 * cap
        outs[k % 2][at : at + cap, :] = dot32(picks, solved).astype(outs[0].dtype)


def pack_rows(index, solved, n_row, cap, after=(), share=0):
    depth = solved[0].shape[0]
    width = sum(part.shape[1] for part in solved)
    return pl.pallas_call(
        functools.partial(pack_kernel, n_row, len(solved)),
        in_specs=[whole_block(*index.shape)]
        + [whole_block(*part.shape) for part in solved]
        + [in_place()] * len(after),
        out_shape=[jax.ShapeDtypeStruct((n_row // 2 * cap, width), solved[0].dtype)] * 2,
        compiler_params=kernel_params(),
        cost_estimate=declared(share * n_row * cap * depth * width),
        name="pack_rows",
    )(index, *solved, *after)


def join_pieces(pieces, joined):
    at = 0
    for piece in pieces:
        joined[at : at + piece.shape[0], :] = piece[...]
        at += piece.shape[0]


def assemble_kernel(n_pieces, index_ref, bem_ref, *refs):
    outs, joined = refs[-3:-1], refs[-1]
    join_pieces(refs[:n_pieces], joined)
    count = outs[0].shape[0]
    step = largest_tile(count, 512)
    for half, out in enumerate(outs):
        for i in range(0, count, step):
            want = index_ref[half * count + i : half * count + i + step, :]
            taken = dot32(one_hot(want, joined.shape[0], joined.dtype), joined[...])
            entries = bem_ref[half, i : i + step, :].astype(jnp.float32)
            out[i : i + step, :] = (entries - taken).astype(out.dtype)


def assemble(index, bem, pieces, start, after=()):
    width = pieces[0].shape[1]
    routed = sum(piece.shape[0] for piece in pieces)
    count = bem.shape[1]
    place = start * TILE // width
    return pl.pallas_call(
        functools.partial(assemble_kernel, len(pieces)),
        grid=(1,),
        in_specs=[
            whole_block(*index.shape),
            pl.BlockSpec((2, count, width), lambda i: (0, 0, place)),
        ]
        + [whole_block(*piece.shape) for piece in pieces]
        + [in_place()] * len(after),
        out_specs=[whole_block(count, width)] * 2,
        out_shape=[jax.ShapeDtypeStruct((count, width), bem.dtype)] * 2,
        scratch_shapes=[pltpu.VMEM((routed, width), bem.dtype)],
        compiler_params=kernel_params(),
        cost_estimate=declared(4 * 2 * count * routed * width),
        name="assemble",
    )(index, bem, *pieces, *after)


def finish_kernel(ready, ready_ref, bem_ref, schur_ref, *refs):
    out = refs[-1]
    out[:, :ready] = ready_ref[...]
    taken = schur_ref[...].astype(jnp.float32)
    out[:, ready:] = (bem_ref[0].astype(jnp.float32) - taken).astype(out.dtype)


def finish(ready, bem, schur, half, after=()):
    (count, width), last = ready.shape, schur.shape[1]
    place = bem.shape[2] // last - 1
    return pl.pallas_call(
        functools.partial(finish_kernel, width),
        grid=(1,),
        in_specs=[
            whole_block(count, width),
            pl.BlockSpec((1, count, last), lambda i: (half, 0, place)),
            whole_block(count, last),
        ]
        + [in_place()] * len(after),
        out_specs=whole_block(count, width + last),
        out_shape=jax.ShapeDtypeStruct((count, width + last), bem.dtype),
        compiler_params=kernel_params(),
        cost_estimate=declared(),
        name="finish",
    )(ready, bem, schur, *after)


def join_kernel(n_parts, *refs):
    join_pieces(refs[:n_parts], refs[-1])


def join(parts, after=()):
    depth, width = sum(part.shape[0] for part in parts), parts[0].shape[1]
    return pl.pallas_call(
        functools.partial(join_kernel, len(parts)),
        in_specs=[whole_block(*part.shape) for part in parts] + [in_place()] * len(after),
        out_shape=jax.ShapeDtypeStruct((depth, width), parts[0].dtype),
        compiler_params=kernel_params(),
        cost_estimate=declared(),
        name="join",
    )(*parts, *after)


def unpack_kernel(n_pieces, n_col, parts, index_ref, *refs):
    outs, joined = refs[-1 - parts : -1], refs[-1]
    join_pieces(refs[:n_pieces], joined)
    _, count, width = outs[0].shape
    step = largest_tile(count, 512)
    for p, out in enumerate(outs):
        for i in range(0, count, step):
            want = index_ref[p * count + i : p * count + i + step, :]
            taken = dot32(one_hot(want, joined.shape[0], joined.dtype), joined[...])
            for d in range(n_col):
                out[d, i : i + step, :] = taken[:, d * width : (d + 1) * width].astype(out.dtype)


def unpack(index, pieces, n_col, parts, after=(), share=0):
    wide = pieces[0].shape[1]
    routed = sum(piece.shape[0] for piece in pieces)
    count, width = index.shape[0] // parts, wide // n_col
    return pl.pallas_call(
        functools.partial(unpack_kernel, len(pieces), n_col, parts),
        in_specs=[whole_block(*index.shape)]
        + [whole_block(*piece.shape) for piece in pieces]
        + [in_place()] * len(after),
        out_shape=[jax.ShapeDtypeStruct((n_col, count, width), pieces[0].dtype)] * parts,
        scratch_shapes=[pltpu.VMEM((routed, wide), pieces[0].dtype)],
        compiler_params=kernel_params(),
        cost_estimate=declared(share * parts * count * routed * wide),
        name="unpack",
    )(index, *pieces, *after)


def product_kernel(streams, minus, order_ref, *refs):
    blocks, (near_ref, far_ref) = refs[:streams], refs[streams : streams + 2]
    out_ref, acc = refs[-2:]
    k = pl.program_id(0)
    steps = pl.num_programs(0)
    half = steps // 2
    deep = near_ref.shape[0] // half

    def term(rows_ref, at):
        matrix = jnp.concatenate([block[...] for block in blocks], axis=1)
        return dot32(matrix, rows_ref[pl.ds(pl.multiple_of(at * deep, deep), deep), :])

    @pl.when(k == 0)
    def _():
        acc[...] = term(near_ref, 0)

    @pl.when((k > 0) & (k < half))
    def _():
        acc[...] += term(near_ref, k)

    @pl.when(k >= half)
    def _():
        acc[...] += term(far_ref, k - half)

    @pl.when(k == steps - 1)
    def _():
        total = acc[...]
        if minus:
            total = refs[streams + 2][...].astype(jnp.float32) - total
        out_ref[...] = total.astype(out_ref.dtype)


def product(matrix, order, near, far, base=None, after=()):
    rows, depth = matrix.shape
    width = near.shape[1]
    n_row = order.shape[0]
    deep = depth // n_row
    streams = 4 if deep % (4 * TILE) == 0 else 1
    bases = [] if base is None else [base]

    def block_of(q):
        return pl.BlockSpec((rows, deep // streams), lambda k, order: (0, order[k] * streams + q))

    return pl.pallas_call(
        functools.partial(product_kernel, streams, bool(bases)),
        grid_spec=pltpu.PrefetchScalarGridSpec(
            num_scalar_prefetch=1,
            grid=(n_row,),
            in_specs=[block_of(q) for q in range(streams)]
            + [whole_block(*near.shape)] * 2
            + [whole_block(rows, width)] * len(bases)
            + [in_place()] * len(after),
            out_specs=whole_block(rows, width),
            scratch_shapes=[pltpu.VMEM((rows, width), jnp.float32)],
        ),
        out_shape=jax.ShapeDtypeStruct((rows, width), near.dtype),
        compiler_params=kernel_params(),
        cost_estimate=declared(6 * rows * depth * max(width, 256)),
        name="product",
    )(order, *[matrix] * streams, near, far, *bases, *after)


def exchange(value, distance, n, axis="row"):
    return lax.ppermute(value, axis, [(i, i ^ distance) for i in range(n)])


def route(packed, n_row):
    near, far = packed[0], exchange(packed[1], 1, n_row)
    cap = near.shape[0] * 2 // n_row
    sent = []
    for i in range(1, n_row // 2):
        both = [near[i * cap : (i + 1) * cap], far[i * cap : (i + 1) * cap]]
        sent.append(jnp.concatenate(both, axis=0))
    pieces = [exchange(both, 2 * i, n_row) for i, both in enumerate(sent, 1)]
    return [near[:cap], far[:cap]] + pieces, tuple(sent)


def gather_rows(block, n_row):
    return [block] + [exchange(block, k, n_row) for k in range(2, n_row, 2)]


def both_cores(near, n_row):
    return near, exchange(near, 1, n_row)


def route_tables(surface_map, rows, n_row, cap, slots):
    me = lax.axis_index("row")
    mine = surface_map.reshape(-1)
    every = lax.all_gather(mine, "row")
    partners = me ^ jnp.arange(n_row, dtype=jnp.int32)
    local = every[partners] - me * rows
    asked = (local >= 0) & (local < rows)
    rank = jnp.cumsum(asked.astype(jnp.int32), axis=1) - 1
    numbers = jnp.arange(slots, dtype=jnp.int32)
    hit = asked[:, None, :] & (rank[:, None, :] == numbers[None, :, None])
    wanted = jnp.sum(jnp.where(hit, local[:, None, :] + 1, 0), axis=2) - 1
    owner = mine // rows
    held = owner[None, :] == jnp.arange(n_row, dtype=jnp.int32)[:, None]
    place = jnp.cumsum(held.astype(jnp.int32), axis=1) - 1
    slot = jnp.sum(jnp.where(held, place, 0), axis=0)
    lands = (owner ^ me) * slots + slot
    return wanted.reshape(-1, 1), lands.reshape(-1, 1)


def per_device(
    front_inverse,
    coupling_tiles,
    tile_row,
    tile_col,
    surface_map,
    bem_entries,
    pivot_inverse,
    slab_below,
):
    n_row, n_col = lax.axis_size("row"), lax.axis_size("col")
    assert n_row > 1 and n_row & (n_row - 1) == 0
    rows, depth = front_inverse.shape
    count = bem_entries.shape[1]
    per_dest = bem_entries.shape[2] // TILE
    cap = rows // n_row
    slots = -(-cap // 16) * 16
    me = lax.axis_index("row")

    col_at = lax.axis_index("col")
    block_row = tile_row - col_at * (depth // TILE)
    dest, sub = tile_col // per_dest, tile_col % per_dest
    meta = jnp.stack([block_row, dest, sub])
    order = me ^ jnp.concatenate(
        [jnp.arange(0, n_row, 2, dtype=jnp.int32), jnp.arange(1, n_row, 2, dtype=jnp.int32)]
    )
    assert per_dest >= 3

    def summed(parts):
        return lax.psum_scatter(parts, "col", scatter_dimension=0)

    def products_of(subs, flats, after):
        return front_products(front_inverse, coupling_tiles, meta, subs, flats, n_col, after)

    last = per_dest - 1
    parts = products_of((0,), (False,), ())
    sums = [summed(parts[0])]
    parts = products_of((1, last), (False, True), (parts[0],))
    sums.append(summed(parts[0]))
    wanted, lands = route_tables(surface_map, rows, n_row, cap, slots)
    packed = pack_rows(wanted, [parts[1]], n_row, slots)
    pieces, after = route(packed, n_row)
    parts = products_of(tuple(range(2, last)), (False,) * (last - 2), after)
    sums += [summed(part) for part in parts]
    upper_last, lower_last = unpack(lands, pieces, n_col, 2, (parts[0],))
    after = (upper_last,)
    upper_last, lower_last = summed(upper_last), summed(lower_last)

    packed = pack_rows(wanted, sums[:2], n_row, slots, after)
    upper, lower = assemble(lands, bem_entries, route(packed, n_row)[0], 0, after)
    first = gather_rows(upper, n_row)
    packed = pack_rows(wanted, sums[2:], n_row, slots, (upper,))
    pieces, after = route(packed, n_row)
    near, far = both_cores(join(first, (packed[0],)), n_row)
    pivots = [product(pivot_inverse, order, near, far, after=after)]
    first = gather_rows(pivots[0], n_row)
    upper, below = assemble(lands, bem_entries, pieces, 2, (pivots[0],))
    upper = finish(upper, bem_entries, upper_last, 0)
    second = gather_rows(upper, n_row)
    near, far = both_cores(join(first, (upper,)), n_row)
    belows = [product(slab_below, order, near, far, lower, (upper,))]
    near, far = both_cores(join(second, (belows[0],)), n_row)
    pivots.append(product(pivot_inverse, order, near, far, after=(belows[0],)))
    second = gather_rows(pivots[1], n_row)
    below = finish(below, bem_entries, lower_last, 1, (pivots[1],))
    near, far = both_cores(join(second, (below,)), n_row)
    belows.append(product(slab_below, order, near, far, below))
    return jnp.stack([jnp.concatenate(parts, axis=1) for parts in (pivots, belows)])


def solution(mesh):
    placed = (
        P("row", "col"),
        P("col", None, None),
        P("col"),
        P("col"),
        P(None, "row"),
        P(None, "row", "col"),
        P("row", None),
        P("row", None),
    )
    return jax.shard_map(
        per_device, mesh=mesh, in_specs=placed, out_specs=P(None, "row", "col"), check_vma=False
    )
```

```python
import functools

import jax
import jax.numpy as jnp
from jax import lax
from jax.experimental import pallas as pl
from jax.experimental.pallas import tpu as pltpu
from jax.sharding import PartitionSpec as P

TILE = 128
STACK = 4
REPEATS = 32
VMEM_BYTES = 56 * 1024 * 1024


def largest_tile(total, most):
    best = total
    for size in range(16, most + 1, 16):
        if total % size == 0:
            best = size
    return best


def kernel_params():
    return pltpu.CompilerParams(vmem_limit_bytes=VMEM_BYTES)


def declared(flops=0):
    return pl.CostEstimate(flops=flops, bytes_accessed=1, transcendentals=0)


def whole_block(*shape):
    return pl.BlockSpec(shape, lambda *_: (0,) * len(shape))


def in_place():
    return pl.BlockSpec(memory_space=pl.ANY)


def dot32(left, right):
    return jnp.dot(left, right, preferred_element_type=jnp.float32)


def front_kernel(subs, flats, n_col, n_after, meta_ref, tiles_ref, front_ref, *refs):
    outs = refs[n_after : n_after + len(subs)]
    stack, held, acc, places, filled, pair_of, state, found, tile_sems, sems = refs[
        n_after + len(subs) :
    ]
    pairs = n_col * len(subs) // 2
    depth_blocks = found.shape[1]
    block, streams = held.shape[1], sems.shape[1]
    lines = block // streams
    step = pl.program_id(0)
    slot = lax.rem(step, 2)

    def front_copy(at, into, q):
        return pltpu.make_async_copy(
            front_ref.at[pl.ds(pl.multiple_of(at * block + q * lines, lines), lines), :],
            held.at[into, pl.ds(q * lines, lines), :],
            sems.at[into, q],
        )

    def half_of(item, place, side):
        rows = pl.ds(pl.multiple_of(place * TILE, TILE), TILE)
        return stack.at[side, item, rows, :]

    def tile_copy(t, item, place, side):
        return pltpu.make_async_copy(
            tiles_ref.at[t], half_of(item, place, side), tile_sems.at[t]
        )

    def chosen(t):
        return functools.reduce(jnp.logical_or, [meta_ref[2, t] == sub for sub in subs])

    def group_of(t):
        order = 0
        for p in range(1, len(subs)):
            order = jnp.where(meta_ref[2, t] == subs[p], p, order)
        return order * n_col + meta_ref[1, t]

    @pl.when(step == 0)
    def build():
        for q in range(streams):
            front_copy(0, 0, q).start()
        for i in range(2 * pairs + 1):
            state[i] = 0

        @pl.loop(0, depth_blocks)
        def forget(row):
            for pair in range(pairs):
                found[pair, row] = -1

        @pl.loop(0, filled.shape[0])
        def empty(item):
            pair_of[item] = 0
            for place in range(STACK):
                places[item, place] = 0
                filled[item, place] = 0

        @pl.loop(0, tiles_ref.shape[0])
        def place_tile(t):
            @pl.when(chosen(t))
            def _():
                g, row = group_of(t), meta_ref[0, t]
                pair, side = lax.div(g, 2), lax.rem(g, 2)

                @pl.when(found[pair, row] < 0)
                def _():
                    at = state[pair]

                    @pl.when(lax.rem(at, STACK) == 0)
                    def _():
                        state[pairs + pair] = state[2 * pairs]
                        pair_of[state[2 * pairs]] = pair
                        state[2 * pairs] += 1

                    item, place = state[pairs + pair], lax.rem(at, STACK)
                    places[item, place] = row
                    found[pair, row] = item * STACK + place
                    state[pair] = at + 1

                item = lax.div(found[pair, row], STACK)
                place = lax.rem(found[pair, row], STACK)
                filled[item, place] += 1 + side
                tile_copy(t, item, place, side).start()

        items = state[2 * pairs]

        @pl.loop(0, (items + 1) // 2 * 2)
        def clear(item):
            for place in range(STACK):
                for side in range(2):

                    @pl.when((filled[item, place] == 0) | (filled[item, place] == 2 - side))
                    def _():
                        half_of(item, place, side)[...] = jnp.zeros((TILE, TILE), stack.dtype)

        @pl.loop(0, tiles_ref.shape[0])
        def wait_tile(t):
            @pl.when(chosen(t))
            def _():
                tile_copy(t, 0, 0, 0).wait()

    @pl.when(step + 1 < pl.num_programs(0))
    def ahead():
        for q in range(streams):
            front_copy(step + 1, 1 - slot, q).start()

    for q in range(streams):
        front_copy(step, slot, q).wait()

    acc[...] = jnp.zeros_like(acc)

    @pl.loop(0, (state[2 * pairs] + 1) // 2)
    def add(s):
        for i in range(2):
            item = s * 2 + i
            lefts = [pl.multiple_of(places[item, j] * TILE, TILE) for j in range(STACK)]
            rows = [held[slot, :, pl.ds(left, TILE)] for left in lefts]
            tiles = jnp.concatenate([stack[0, item], stack[1, item]], axis=1)
            acc[pair_of[item]] += dot32(jnp.concatenate(rows, axis=1), tiles)

    for g in range(2 * pairs):
        out, dest = outs[g // n_col], g % n_col
        value = acc[g // 2, :, g % 2 * TILE : (g % 2 + 1) * TILE].astype(out.dtype)
        if flats[g // n_col]:
            out[:, dest * TILE : (dest + 1) * TILE] = value
        else:
            out[dest] = value


def front_products(front, tiles, meta, subs, flats, n_col, after=()):
    rows, depth = front.shape
    pairs = n_col * len(subs) // 2
    block = largest_tile(rows, 512)
    streams = 8 if block % 128 == 0 else 1
    count = tiles.shape[0]
    items = (-(-count // STACK) + pairs + 2) // 2 * 2
    shapes, specs = [], []
    for flat in flats:
        if flat:
            shapes.append((rows, n_col * TILE))
            specs.append(pl.BlockSpec((block, n_col * TILE), lambda i, m: (i, 0)))
        else:
            shapes.append((n_col, rows, TILE))
            specs.append(pl.BlockSpec((n_col, block, TILE), lambda i, m: (0, i, 0)))
    return pl.pallas_call(
        functools.partial(front_kernel, subs, flats, n_col, len(after)),
        grid_spec=pltpu.PrefetchScalarGridSpec(
            num_scalar_prefetch=1,
            grid=(rows // block,),
            in_specs=[in_place()] * (2 + len(after)),
            out_specs=specs,
            scratch_shapes=[
                pltpu.VMEM((2, items, STACK * TILE, TILE), front.dtype),
                pltpu.VMEM((2, block, depth), front.dtype),
                pltpu.VMEM((pairs, block, 2 * TILE), jnp.float32),
                pltpu.SMEM((items, STACK), jnp.int32),
                pltpu.SMEM((items, STACK), jnp.int32),
                pltpu.SMEM((items,), jnp.int32),
                pltpu.SMEM((2 * pairs + 1,), jnp.int32),
                pltpu.SMEM((pairs, depth // TILE), jnp.int32),
                pltpu.SemaphoreType.DMA((count,)),
                pltpu.SemaphoreType.DMA((2, streams)),
            ],
        ),
        out_shape=[jax.ShapeDtypeStruct(shape, front.dtype) for shape in shapes],
        compiler_params=kernel_params(),
        cost_estimate=declared(),
        name="front_products",
    )(meta, tiles, front, *after)


def one_hot(want, depth, kind):
    places = lax.broadcasted_iota(jnp.int32, (want.shape[0], depth), 1)
    return (places == want).astype(jnp.float32).astype(kind)


def pack_kernel(n_row, n_solved, index_ref, *refs):
    outs = refs[-2:]
    solved = jnp.concatenate([ref[...] for ref in refs[:n_solved]], axis=1)
    cap = outs[0].shape[0] * 2 // n_row
    for k in range(n_row):
        picks = one_hot(index_ref[k * cap : (k + 1) * cap, :], solved.shape[0], solved.dtype)
        at = k // 2 * cap
        outs[k % 2][at : at + cap, :] = dot32(picks, solved).astype(outs[0].dtype)


def pack_rows(index, solved, n_row, cap, after=(), share=0):
    depth = solved[0].shape[0]
    width = sum(part.shape[1] for part in solved)
    return pl.pallas_call(
        functools.partial(pack_kernel, n_row, len(solved)),
        in_specs=[whole_block(*index.shape)]
        + [whole_block(*part.shape) for part in solved]
        + [in_place()] * len(after),
        out_shape=[jax.ShapeDtypeStruct((n_row // 2 * cap, width), solved[0].dtype)] * 2,
        compiler_params=kernel_params(),
        cost_estimate=declared(share * n_row * cap * depth * width),
        name="pack_rows",
    )(index, *solved, *after)


def join_pieces(pieces, joined):
    at = 0
    for piece in pieces:
        joined[at : at + piece.shape[0], :] = piece[...]
        at += piece.shape[0]


def assemble_kernel(n_pieces, index_ref, bem_ref, *refs):
    outs, joined = refs[-3:-1], refs[-1]
    join_pieces(refs[:n_pieces], joined)
    count = outs[0].shape[0]
    step = largest_tile(count, 512)
    for half, out in enumerate(outs):
        for i in range(0, count, step):
            want = index_ref[half * count + i : half * count + i + step, :]
            taken = dot32(one_hot(want, joined.shape[0], joined.dtype), joined[...])
            entries = bem_ref[half, i : i + step, :].astype(jnp.float32)
            out[i : i + step, :] = (entries - taken).astype(out.dtype)


def assemble(index, bem, pieces, start, after=()):
    width = pieces[0].shape[1]
    routed = sum(piece.shape[0] for piece in pieces)
    count = bem.shape[1]
    place = start * TILE // width
    return pl.pallas_call(
        functools.partial(assemble_kernel, len(pieces)),
        grid=(1,),
        in_specs=[
            whole_block(*index.shape),
            pl.BlockSpec((2, count, width), lambda i: (0, 0, place)),
        ]
        + [whole_block(*piece.shape) for piece in pieces]
        + [in_place()] * len(after),
        out_specs=[whole_block(count, width)] * 2,
        out_shape=[jax.ShapeDtypeStruct((count, width), bem.dtype)] * 2,
        scratch_shapes=[pltpu.VMEM((routed, width), bem.dtype)],
        compiler_params=kernel_params(),
        cost_estimate=declared(4 * 2 * count * routed * width),
        name="assemble",
    )(index, bem, *pieces, *after)


def subtract_kernel(n_parts, bem_ref, *refs):
    out = refs[-1]
    for at, part in enumerate(refs[:n_parts]):
        columns = slice(at * TILE, (at + 1) * TILE)
        taken = part[...].astype(jnp.float32)
        out[:, columns] = (bem_ref[0, :, columns].astype(jnp.float32) - taken).astype(out.dtype)


def subtract(bem, parts, half, start, after=()):
    count, width = bem.shape[1], len(parts) * TILE
    place = start * TILE // width

    def rows_of(part):
        at = half if part.shape[0] > count else 0
        return pl.BlockSpec((count, TILE), lambda i: (at, 0))

    return pl.pallas_call(
        functools.partial(subtract_kernel, len(parts)),
        grid=(1,),
        in_specs=[pl.BlockSpec((1, count, width), lambda i: (half, 0, place))]
        + [rows_of(part) for part in parts]
        + [in_place()] * len(after),
        out_specs=whole_block(count, width),
        out_shape=jax.ShapeDtypeStruct((count, width), bem.dtype),
        compiler_params=kernel_params(),
        cost_estimate=declared(),
        name="subtract",
    )(bem, *parts, *after)


def join_kernel(n_parts, *refs):
    join_pieces(refs[:n_parts], refs[-1])


def join(parts, after=()):
    depth, width = sum(part.shape[0] for part in parts), parts[0].shape[1]
    return pl.pallas_call(
        functools.partial(join_kernel, len(parts)),
        in_specs=[whole_block(*part.shape) for part in parts] + [in_place()] * len(after),
        out_shape=jax.ShapeDtypeStruct((depth, width), parts[0].dtype),
        compiler_params=kernel_params(),
        cost_estimate=declared(),
        name="join",
    )(*parts, *after)


def unpack_kernel(n_pieces, n_col, parts, index_ref, *refs):
    outs, joined = refs[-1 - parts : -1], refs[-1]
    join_pieces(refs[:n_pieces], joined)
    _, count, width = outs[0].shape
    step = largest_tile(count, 512)
    for p, out in enumerate(outs):
        for i in range(0, count, step):
            want = index_ref[p * count + i : p * count + i + step, :]
            taken = dot32(one_hot(want, joined.shape[0], joined.dtype), joined[...])
            for d in range(n_col):
                out[d, i : i + step, :] = taken[:, d * width : (d + 1) * width].astype(out.dtype)


def unpack(index, pieces, n_col, parts, after=(), share=0):
    wide = pieces[0].shape[1]
    routed = sum(piece.shape[0] for piece in pieces)
    count, width = index.shape[0] // parts, wide // n_col
    return pl.pallas_call(
        functools.partial(unpack_kernel, len(pieces), n_col, parts),
        in_specs=[whole_block(*index.shape)]
        + [whole_block(*piece.shape) for piece in pieces]
        + [in_place()] * len(after),
        out_shape=[jax.ShapeDtypeStruct((n_col, count, width), pieces[0].dtype)] * parts,
        scratch_shapes=[pltpu.VMEM((routed, wide), pieces[0].dtype)],
        compiler_params=kernel_params(),
        cost_estimate=declared(share * parts * count * routed * wide),
        name="unpack",
    )(index, *pieces, *after)


def product_kernel(streams, minus, order_ref, *refs):
    blocks, (near_ref, far_ref) = refs[:streams], refs[streams : streams + 2]
    out_ref, acc = refs[-2:]
    k = pl.program_id(0)
    steps = pl.num_programs(0)
    half = steps // 2
    deep = near_ref.shape[0] // half

    def term(rows_ref, at):
        matrix = jnp.concatenate([block[...] for block in blocks], axis=1)
        return dot32(matrix, rows_ref[pl.ds(pl.multiple_of(at * deep, deep), deep), :])

    @pl.when(k == 0)
    def _():
        acc[...] = term(near_ref, 0)

    @pl.when((k > 0) & (k < half))
    def _():
        acc[...] += term(near_ref, k)

    @pl.when(k >= half)
    def _():
        acc[...] += term(far_ref, k - half)

    @pl.when(k == steps - 1)
    def _():
        total = acc[...]
        if minus:
            total = refs[streams + 2][...].astype(jnp.float32) - total
        out_ref[...] = total.astype(out_ref.dtype)


def product(matrix, order, near, far, base=None, after=()):
    rows, depth = matrix.shape
    width = near.shape[1]
    n_row = order.shape[0]
    deep = depth // n_row
    streams = 4 if deep % (4 * TILE) == 0 else 1
    bases = [] if base is None else [base]

    def block_of(q):
        return pl.BlockSpec((rows, deep // streams), lambda k, order: (0, order[k] * streams + q))

    return pl.pallas_call(
        functools.partial(product_kernel, streams, bool(bases)),
        grid_spec=pltpu.PrefetchScalarGridSpec(
            num_scalar_prefetch=1,
            grid=(n_row,),
            in_specs=[block_of(q) for q in range(streams)]
            + [whole_block(*near.shape)] * 2
            + [whole_block(rows, width)] * len(bases)
            + [in_place()] * len(after),
            out_specs=whole_block(rows, width),
            scratch_shapes=[pltpu.VMEM((rows, width), jnp.float32)],
        ),
        out_shape=jax.ShapeDtypeStruct((rows, width), near.dtype),
        compiler_params=kernel_params(),
        cost_estimate=declared(6 * rows * depth * max(width, 256)),
        name="product",
    )(order, *[matrix] * streams, near, far, *bases, *after)


def exchange(value, distance, n, axis="row"):
    return lax.ppermute(value, axis, [(i, i ^ distance) for i in range(n)])


def route(packed, n_row):
    near, far = packed[0], exchange(packed[1], 1, n_row)
    cap = near.shape[0] * 2 // n_row
    sent = []
    for i in range(1, n_row // 2):
        both = [near[i * cap : (i + 1) * cap], far[i * cap : (i + 1) * cap]]
        sent.append(jnp.concatenate(both, axis=0))
    pieces = [exchange(both, 2 * i, n_row) for i, both in enumerate(sent, 1)]
    return [near[:cap], far[:cap]] + pieces, tuple(sent)


def gather_rows(block, n_row):
    return [block] + [exchange(block, k, n_row) for k in range(2, n_row, 2)]


def both_cores(near, n_row):
    return near, exchange(near, 1, n_row)


def route_tables(surface_map, rows, n_row, cap, slots):
    me = lax.axis_index("row")
    mine = surface_map.reshape(-1)
    shifts = jnp.arange(REPEATS, dtype=jnp.int32)[:, None]
    every = lax.all_gather(mine[None, :] + shifts, "row")[:, 0]
    partners = me ^ jnp.arange(n_row, dtype=jnp.int32)
    local = every[partners] - me * rows
    asked = (local >= 0) & (local < rows)
    rank = jnp.cumsum(asked.astype(jnp.int32), axis=1) - 1
    numbers = jnp.arange(slots, dtype=jnp.int32)
    hit = asked[:, None, :] & (rank[:, None, :] == numbers[None, :, None])
    wanted = jnp.sum(jnp.where(hit, local[:, None, :] + 1, 0), axis=2) - 1
    owner = mine // rows
    held = owner[None, :] == jnp.arange(n_row, dtype=jnp.int32)[:, None]
    place = jnp.cumsum(held.astype(jnp.int32), axis=1) - 1
    slot = jnp.sum(jnp.where(held, place, 0), axis=0)
    lands = (owner ^ me) * slots + slot
    return wanted.reshape(-1, 1), lands.reshape(-1, 1)


def per_device(
    front_inverse,
    coupling_tiles,
    tile_row,
    tile_col,
    surface_map,
    bem_entries,
    pivot_inverse,
    slab_below,
):
    n_row, n_col = lax.axis_size("row"), lax.axis_size("col")
    assert n_row > 1 and n_row & (n_row - 1) == 0
    rows, depth = front_inverse.shape
    count = bem_entries.shape[1]
    per_dest = bem_entries.shape[2] // TILE
    cap = rows // n_row
    slots = -(-cap // 16) * 16
    me = lax.axis_index("row")

    col_at = lax.axis_index("col")
    block_row = tile_row - col_at * (depth // TILE)
    dest, sub = tile_col // per_dest, tile_col % per_dest
    meta = jnp.stack([block_row, dest, sub])
    order = me ^ jnp.concatenate(
        [jnp.arange(0, n_row, 2, dtype=jnp.int32), jnp.arange(1, n_row, 2, dtype=jnp.int32)]
    )
    half = per_dest // 2
    assert per_dest == 2 * half

    def summed(parts):
        return lax.psum_scatter(parts, "col", scatter_dimension=0)

    parts = front_products(
        front_inverse, coupling_tiles, meta, tuple(range(half)), (False,) * half, n_col
    )
    solved = [summed(part) for part in parts]
    flats = front_products(
        front_inverse, coupling_tiles, meta, tuple(range(half, per_dest)), (True,) * half, n_col,
        (parts[0],),
    )
    wanted, lands = route_tables(surface_map, rows, n_row, cap, slots)
    routed, after = [], ()
    for flat in flats:
        packed = pack_rows(wanted, [flat], n_row, slots, after)
        pieces, after = route(packed, n_row)
        routed.append(pieces)
    after = (packed[0],)

    uppers, lowers = [], []
    for at, pieces in enumerate(routed):
        cuts = unpack(lands, pieces, n_col, 1 if at + 1 < half else 2, after, 12)
        uppers.append(summed(cuts[0]))
        lowers.append(cuts[1:])
        after = (cuts[0],)
        if at == 0:
            packed = pack_rows(wanted, solved, n_row, slots, after, 12)
            after = (packed[0],)
    lowers = [summed(low[0]) if low else both for low, both in zip(lowers, uppers)]

    upper, lower = assemble(lands, bem_entries, route(packed, n_row)[0], 0, after)
    first = gather_rows(upper, n_row)
    upper = subtract(bem_entries, uppers, 0, half, (upper,))
    second = gather_rows(upper, n_row)
    near, far = both_cores(join(first, (upper,)), n_row)
    pivots = [product(pivot_inverse, order, near, far, after=(upper,))]
    first = gather_rows(pivots[0], n_row)
    near, far = both_cores(join(second, (pivots[0],)), n_row)
    pivots.append(product(pivot_inverse, order, near, far, after=(pivots[0],)))
    second = gather_rows(pivots[1], n_row)
    near, far = both_cores(join(first, (pivots[1],)), n_row)
    below = subtract(bem_entries, lowers, 1, half, (pivots[1],))
    belows = [product(slab_below, order, near, far, lower, (below,))]
    near, far = both_cores(join(second, (belows[0],)), n_row)
    belows.append(product(slab_below, order, near, far, below))
    return jnp.stack([jnp.concatenate(parts, axis=1) for parts in (pivots, belows)])


def solution(mesh):
    placed = (
        P("row", "col"),
        P("col", None, None),
        P("col"),
        P("col"),
        P(None, "row"),
        P(None, "row", "col"),
        P("row", None),
        P("row", None),
    )
    return jax.shard_map(
        per_device, mesh=mesh, in_specs=placed, out_specs=P(None, "row", "col"), check_vma=False
    )
```

```python
import functools

import jax
import jax.numpy as jnp
from jax import lax
from jax.experimental import pallas as pl
from jax.experimental.pallas import tpu as pltpu
from jax.sharding import PartitionSpec as P

TILE = 128
STACK = 4
REPEATS = 32
VMEM_BYTES = 56 * 1024 * 1024


def largest_tile(total, most):
    best = total
    for size in range(16, most + 1, 16):
        if total % size == 0:
            best = size
    return best


def kernel_params():
    return pltpu.CompilerParams(vmem_limit_bytes=VMEM_BYTES)


def declared(flops=0):
    return pl.CostEstimate(flops=flops, bytes_accessed=1, transcendentals=0)


def whole_block(*shape):
    return pl.BlockSpec(shape, lambda *_: (0,) * len(shape))


def in_place():
    return pl.BlockSpec(memory_space=pl.ANY)


def dot32(left, right):
    return jnp.dot(left, right, preferred_element_type=jnp.float32)


def front_kernel(subs, flats, n_col, n_after, meta_ref, tiles_ref, front_ref, *refs):
    outs = refs[n_after : n_after + len(subs)]
    stack, held, acc, places, groups_of, state, tile_sems, sems = refs[n_after + len(subs) :]
    groups = n_col * len(subs)
    block, streams = held.shape[1], sems.shape[1]
    lines = block // streams
    step = pl.program_id(0)
    slot = lax.rem(step, 2)

    def front_copy(at, into, q):
        return pltpu.make_async_copy(
            front_ref.at[pl.ds(pl.multiple_of(at * block + q * lines, lines), lines), :],
            held.at[into, pl.ds(q * lines, lines), :],
            sems.at[into, q],
        )

    def tile_copy(t, item, place):
        return pltpu.make_async_copy(
            tiles_ref.at[t],
            stack.at[item, pl.ds(pl.multiple_of(place * TILE, TILE), TILE), :],
            tile_sems.at[t],
        )

    def chosen(t):
        return functools.reduce(jnp.logical_or, [meta_ref[2, t] == sub for sub in subs])

    def group_of(t):
        order = 0
        for p in range(1, len(subs)):
            order = jnp.where(meta_ref[2, t] == subs[p], p, order)
        return order * n_col + meta_ref[1, t]

    def clear(item, place):
        places[item, place] = 0
        stack[item, pl.ds(pl.multiple_of(place * TILE, TILE), TILE), :] = jnp.zeros(
            (TILE, TILE), stack.dtype
        )

    @pl.when(step == 0)
    def build():
        for q in range(streams):
            front_copy(0, 0, q).start()
        for g in range(groups):
            state[g] = 0
            state[groups + g] = 0
        state[2 * groups] = 0

        @pl.loop(0, tiles_ref.shape[0])
        def place_tile(t):
            @pl.when(chosen(t))
            def _():
                g = group_of(t)
                at = state[g]

                @pl.when(lax.rem(at, STACK) == 0)
                def _():
                    state[groups + g] = state[2 * groups]
                    groups_of[state[2 * groups]] = g
                    state[2 * groups] += 1

                item = state[groups + g]
                places[item, lax.rem(at, STACK)] = meta_ref[0, t]
                tile_copy(t, item, lax.rem(at, STACK)).start()
                state[g] = at + 1

        for g in range(groups):
            used = lax.rem(state[g], STACK)

            @pl.loop(used, jnp.where(used == 0, 0, STACK))
            def fill(place):
                clear(state[groups + g], place)

        items = state[2 * groups]

        @pl.loop(items, (items + STACK - 1) // STACK * STACK)
        def fill_item(item):
            groups_of[item] = 0
            for place in range(STACK):
                clear(item, place)

        @pl.loop(0, tiles_ref.shape[0])
        def wait_tile(t):
            @pl.when(chosen(t))
            def _():
                tile_copy(t, 0, 0).wait()

    @pl.when(step + 1 < pl.num_programs(0))
    def ahead():
        for q in range(streams):
            front_copy(step + 1, 1 - slot, q).start()

    for q in range(streams):
        front_copy(step, slot, q).wait()

    acc[...] = jnp.zeros_like(acc)

    @pl.loop(0, (state[2 * groups] + STACK - 1) // STACK)
    def add(s):
        for i in range(STACK):
            item = s * STACK + i
            lefts = [pl.multiple_of(places[item, j] * TILE, TILE) for j in range(STACK)]
            rows = [held[slot, :, pl.ds(left, TILE)] for left in lefts]
            acc[groups_of[item]] += dot32(jnp.concatenate(rows, axis=1), stack[item])

    for g in range(groups):
        out, dest = outs[g // n_col], g % n_col
        if flats[g // n_col]:
            out[:, dest * TILE : (dest + 1) * TILE] = acc[g].astype(out.dtype)
        else:
            out[dest] = acc[g].astype(out.dtype)


def front_products(front, tiles, meta, subs, flats, n_col, after=()):
    rows, depth = front.shape
    groups = n_col * len(subs)
    block = largest_tile(rows, 512)
    streams = 8 if block % 128 == 0 else 1
    count = tiles.shape[0]
    items = (-(-count // STACK) + groups + STACK) // STACK * STACK
    shapes, specs = [], []
    for flat in flats:
        if flat:
            shapes.append((rows, n_col * TILE))
            specs.append(pl.BlockSpec((block, n_col * TILE), lambda i, m: (i, 0)))
        else:
            shapes.append((n_col, rows, TILE))
            specs.append(pl.BlockSpec((n_col, block, TILE), lambda i, m: (0, i, 0)))
    return pl.pallas_call(
        functools.partial(front_kernel, subs, flats, n_col, len(after)),
        grid_spec=pltpu.PrefetchScalarGridSpec(
            num_scalar_prefetch=1,
            grid=(rows // block,),
            in_specs=[in_place()] * (2 + len(after)),
            out_specs=specs,
            scratch_shapes=[
                pltpu.VMEM((items, STACK * TILE, TILE), front.dtype),
                pltpu.VMEM((2, block, depth), front.dtype),
                pltpu.VMEM((groups, block, TILE), jnp.float32),
                pltpu.SMEM((items, STACK), jnp.int32),
                pltpu.SMEM((items,), jnp.int32),
                pltpu.SMEM((2 * groups + 1,), jnp.int32),
                pltpu.SemaphoreType.DMA((count,)),
                pltpu.SemaphoreType.DMA((2, streams)),
            ],
        ),
        out_shape=[jax.ShapeDtypeStruct(shape, front.dtype) for shape in shapes],
        compiler_params=kernel_params(),
        cost_estimate=declared(),
        name="front_products",
    )(meta, tiles, front, *after)


def one_hot(want, depth, kind):
    places = lax.broadcasted_iota(jnp.int32, (want.shape[0], depth), 1)
    return (places == want).astype(jnp.float32).astype(kind)


def pack_kernel(n_row, n_solved, index_ref, *refs):
    outs = refs[-2:]
    solved = jnp.concatenate([ref[...] for ref in refs[:n_solved]], axis=1)
    cap = outs[0].shape[0] * 2 // n_row
    for k in range(n_row):
        picks = one_hot(index_ref[k * cap : (k + 1) * cap, :], solved.shape[0], solved.dtype)
        at = k // 2 * cap
        outs[k % 2][at : at + cap, :] = dot32(picks, solved).astype(outs[0].dtype)


def pack_rows(index, solved, n_row, cap, after=(), share=0):
    depth = solved[0].shape[0]
    width = sum(part.shape[1] for part in solved)
    return pl.pallas_call(
        functools.partial(pack_kernel, n_row, len(solved)),
        in_specs=[whole_block(*index.shape)]
        + [whole_block(*part.shape) for part in solved]
        + [in_place()] * len(after),
        out_shape=[jax.ShapeDtypeStruct((n_row // 2 * cap, width), solved[0].dtype)] * 2,
        compiler_params=kernel_params(),
        cost_estimate=declared(share * n_row * cap * depth * width),
        name="pack_rows",
    )(index, *solved, *after)


def join_pieces(pieces, joined):
    at = 0
    for piece in pieces:
        joined[at : at + piece.shape[0], :] = piece[...]
        at += piece.shape[0]


def assemble_kernel(n_pieces, index_ref, bem_ref, *refs):
    outs, joined = refs[-3:-1], refs[-1]
    join_pieces(refs[:n_pieces], joined)
    count = outs[0].shape[0]
    step = largest_tile(count, 512)
    for half, out in enumerate(outs):
        for i in range(0, count, step):
            want = index_ref[half * count + i : half * count + i + step, :]
            taken = dot32(one_hot(want, joined.shape[0], joined.dtype), joined[...])
            entries = bem_ref[half, i : i + step, :].astype(jnp.float32)
            out[i : i + step, :] = (entries - taken).astype(out.dtype)


def assemble(index, bem, pieces, start, after=()):
    width = pieces[0].shape[1]
    routed = sum(piece.shape[0] for piece in pieces)
    count = bem.shape[1]
    place = start * TILE // width
    return pl.pallas_call(
        functools.partial(assemble_kernel, len(pieces)),
        grid=(1,),
        in_specs=[
            whole_block(*index.shape),
            pl.BlockSpec((2, count, width), lambda i: (0, 0, place)),
        ]
        + [whole_block(*piece.shape) for piece in pieces]
        + [in_place()] * len(after),
        out_specs=[whole_block(count, width)] * 2,
        out_shape=[jax.ShapeDtypeStruct((count, width), bem.dtype)] * 2,
        scratch_shapes=[pltpu.VMEM((routed, width), bem.dtype)],
        compiler_params=kernel_params(),
        cost_estimate=declared(4 * 2 * count * routed * width),
        name="assemble",
    )(index, bem, *pieces, *after)


def subtract_kernel(n_parts, bem_ref, *refs):
    out = refs[-1]
    for at, part in enumerate(refs[:n_parts]):
        columns = slice(at * TILE, (at + 1) * TILE)
        taken = part[...].astype(jnp.float32)
        out[:, columns] = (bem_ref[0, :, columns].astype(jnp.float32) - taken).astype(out.dtype)


def subtract(bem, parts, half, start, after=()):
    count, width = bem.shape[1], len(parts) * TILE
    place = start * TILE // width

    def rows_of(part):
        at = half if part.shape[0] > count else 0
        return pl.BlockSpec((count, TILE), lambda i: (at, 0))

    return pl.pallas_call(
        functools.partial(subtract_kernel, len(parts)),
        grid=(1,),
        in_specs=[pl.BlockSpec((1, count, width), lambda i: (half, 0, place))]
        + [rows_of(part) for part in parts]
        + [in_place()] * len(after),
        out_specs=whole_block(count, width),
        out_shape=jax.ShapeDtypeStruct((count, width), bem.dtype),
        compiler_params=kernel_params(),
        cost_estimate=declared(),
        name="subtract",
    )(bem, *parts, *after)


def finish_kernel(ready, ready_ref, bem_ref, schur_ref, *refs):
    out = refs[-1]
    out[:, :ready] = ready_ref[...]
    taken = schur_ref[...].astype(jnp.float32)
    out[:, ready:] = (bem_ref[0].astype(jnp.float32) - taken).astype(out.dtype)


def finish(ready, bem, schur, half, after=()):
    (count, width), last = ready.shape, schur.shape[1]
    place = bem.shape[2] // last - 1
    return pl.pallas_call(
        functools.partial(finish_kernel, width),
        grid=(1,),
        in_specs=[
            whole_block(count, width),
            pl.BlockSpec((1, count, last), lambda i: (half, 0, place)),
            whole_block(count, last),
        ]
        + [in_place()] * len(after),
        out_specs=whole_block(count, width + last),
        out_shape=jax.ShapeDtypeStruct((count, width + last), bem.dtype),
        compiler_params=kernel_params(),
        cost_estimate=declared(),
        name="finish",
    )(ready, bem, schur, *after)


def join_kernel(n_parts, *refs):
    join_pieces(refs[:n_parts], refs[-1])


def join(parts, after=()):
    depth, width = sum(part.shape[0] for part in parts), parts[0].shape[1]
    return pl.pallas_call(
        functools.partial(join_kernel, len(parts)),
        in_specs=[whole_block(*part.shape) for part in parts] + [in_place()] * len(after),
        out_shape=jax.ShapeDtypeStruct((depth, width), parts[0].dtype),
        compiler_params=kernel_params(),
        cost_estimate=declared(),
        name="join",
    )(*parts, *after)


def unpack_kernel(n_pieces, n_col, parts, index_ref, *refs):
    outs, joined = refs[-1 - parts : -1], refs[-1]
    join_pieces(refs[:n_pieces], joined)
    _, count, width = outs[0].shape
    step = largest_tile(count, 512)
    for p, out in enumerate(outs):
        for i in range(0, count, step):
            want = index_ref[p * count + i : p * count + i + step, :]
            taken = dot32(one_hot(want, joined.shape[0], joined.dtype), joined[...])
            for d in range(n_col):
                out[d, i : i + step, :] = taken[:, d * width : (d + 1) * width].astype(out.dtype)


def unpack(index, pieces, n_col, parts, after=(), share=0):
    wide = pieces[0].shape[1]
    routed = sum(piece.shape[0] for piece in pieces)
    count, width = index.shape[0] // parts, wide // n_col
    return pl.pallas_call(
        functools.partial(unpack_kernel, len(pieces), n_col, parts),
        in_specs=[whole_block(*index.shape)]
        + [whole_block(*piece.shape) for piece in pieces]
        + [in_place()] * len(after),
        out_shape=[jax.ShapeDtypeStruct((n_col, count, width), pieces[0].dtype)] * parts,
        scratch_shapes=[pltpu.VMEM((routed, wide), pieces[0].dtype)],
        compiler_params=kernel_params(),
        cost_estimate=declared(share * parts * count * routed * wide),
        name="unpack",
    )(index, *pieces, *after)


def product_kernel(streams, minus, order_ref, *refs):
    blocks, (near_ref, far_ref) = refs[:streams], refs[streams : streams + 2]
    out_ref, acc = refs[-2:]
    k = pl.program_id(0)
    steps = pl.num_programs(0)
    half = steps // 2
    deep = near_ref.shape[0] // half

    def term(rows_ref, at):
        matrix = jnp.concatenate([block[...] for block in blocks], axis=1)
        return dot32(matrix, rows_ref[pl.ds(pl.multiple_of(at * deep, deep), deep), :])

    @pl.when(k == 0)
    def _():
        acc[...] = term(near_ref, 0)

    @pl.when((k > 0) & (k < half))
    def _():
        acc[...] += term(near_ref, k)

    @pl.when(k >= half)
    def _():
        acc[...] += term(far_ref, k - half)

    @pl.when(k == steps - 1)
    def _():
        total = acc[...]
        if minus:
            total = refs[streams + 2][...].astype(jnp.float32) - total
        out_ref[...] = total.astype(out_ref.dtype)


def product(matrix, order, near, far, base=None, after=()):
    rows, depth = matrix.shape
    width = near.shape[1]
    n_row = order.shape[0]
    deep = depth // n_row
    streams = 4 if deep % (4 * TILE) == 0 else 1
    bases = [] if base is None else [base]

    def block_of(q):
        return pl.BlockSpec((rows, deep // streams), lambda k, order: (0, order[k] * streams + q))

    return pl.pallas_call(
        functools.partial(product_kernel, streams, bool(bases)),
        grid_spec=pltpu.PrefetchScalarGridSpec(
            num_scalar_prefetch=1,
            grid=(n_row,),
            in_specs=[block_of(q) for q in range(streams)]
            + [whole_block(*near.shape)] * 2
            + [whole_block(rows, width)] * len(bases)
            + [in_place()] * len(after),
            out_specs=whole_block(rows, width),
            scratch_shapes=[pltpu.VMEM((rows, width), jnp.float32)],
        ),
        out_shape=jax.ShapeDtypeStruct((rows, width), near.dtype),
        compiler_params=kernel_params(),
        cost_estimate=declared(6 * rows * depth * max(width, 256)),
        name="product",
    )(order, *[matrix] * streams, near, far, *bases, *after)


def exchange(value, distance, n, axis="row"):
    return lax.ppermute(value, axis, [(i, i ^ distance) for i in range(n)])


def route(packed, n_row):
    near, far = packed[0], exchange(packed[1], 1, n_row)
    cap = near.shape[0] * 2 // n_row
    sent = []
    for i in range(1, n_row // 2):
        both = [near[i * cap : (i + 1) * cap], far[i * cap : (i + 1) * cap]]
        sent.append(jnp.concatenate(both, axis=0))
    pieces = [exchange(both, 2 * i, n_row) for i, both in enumerate(sent, 1)]
    return [near[:cap], far[:cap]] + pieces, tuple(sent)


def gather_rows(block, n_row):
    return [block] + [exchange(block, k, n_row) for k in range(2, n_row, 2)]


def both_cores(near, n_row):
    return near, exchange(near, 1, n_row)


def route_tables(surface_map, rows, n_row, cap, slots):
    me = lax.axis_index("row")
    mine = surface_map.reshape(-1)
    shifts = jnp.arange(REPEATS, dtype=jnp.int32)[:, None]
    every = lax.all_gather(mine[None, :] + shifts, "row")[:, 0]
    partners = me ^ jnp.arange(n_row, dtype=jnp.int32)
    local = every[partners] - me * rows
    asked = (local >= 0) & (local < rows)
    rank = jnp.cumsum(asked.astype(jnp.int32), axis=1) - 1
    numbers = jnp.arange(slots, dtype=jnp.int32)
    hit = asked[:, None, :] & (rank[:, None, :] == numbers[None, :, None])
    wanted = jnp.sum(jnp.where(hit, local[:, None, :] + 1, 0), axis=2) - 1
    owner = mine // rows
    held = owner[None, :] == jnp.arange(n_row, dtype=jnp.int32)[:, None]
    place = jnp.cumsum(held.astype(jnp.int32), axis=1) - 1
    slot = jnp.sum(jnp.where(held, place, 0), axis=0)
    lands = (owner ^ me) * slots + slot
    return wanted.reshape(-1, 1), lands.reshape(-1, 1)


def per_device(
    front_inverse,
    coupling_tiles,
    tile_row,
    tile_col,
    surface_map,
    bem_entries,
    pivot_inverse,
    slab_below,
):
    n_row, n_col = lax.axis_size("row"), lax.axis_size("col")
    assert n_row > 1 and n_row & (n_row - 1) == 0
    rows, depth = front_inverse.shape
    count = bem_entries.shape[1]
    per_dest = bem_entries.shape[2] // TILE
    cap = rows // n_row
    slots = -(-cap // 16) * 16
    me = lax.axis_index("row")

    col_at = lax.axis_index("col")
    block_row = tile_row - col_at * (depth // TILE)
    dest, sub = tile_col // per_dest, tile_col % per_dest
    meta = jnp.stack([block_row, dest, sub])
    order = me ^ jnp.concatenate(
        [jnp.arange(0, n_row, 2, dtype=jnp.int32), jnp.arange(1, n_row, 2, dtype=jnp.int32)]
    )
    half = per_dest // 2
    assert per_dest == 2 * half

    def summed(parts):
        return lax.psum_scatter(parts, "col", scatter_dimension=0)

    parts = front_products(
        front_inverse, coupling_tiles, meta, tuple(range(half)), (False,) * half, n_col
    )
    solved = [summed(part) for part in parts]
    flats = front_products(
        front_inverse, coupling_tiles, meta, tuple(range(half, per_dest)), (True,) * half, n_col,
        (parts[0],),
    )
    wanted, lands = route_tables(surface_map, rows, n_row, cap, slots)
    routed, after = [], ()
    for flat in flats:
        packed = pack_rows(wanted, [flat], n_row, slots, after)
        pieces, after = route(packed, n_row)
        routed.append(pieces)
    after = (packed[0],)

    uppers, lowers = [], []
    for at, pieces in enumerate(routed):
        cuts = unpack(lands, pieces, n_col, 1 if at + 1 < half else 2, after, 12)
        uppers.append(summed(cuts[0]))
        lowers.append(cuts[1:])
        after = (cuts[0],)
        if at == 0:
            packed = pack_rows(wanted, solved, n_row, slots, after, 12)
            after = (packed[0],)
    lowers = [summed(low[0]) if low else both for low, both in zip(lowers, uppers)]

    upper, lower = assemble(lands, bem_entries, route(packed, n_row)[0], 0, after)
    first = gather_rows(upper, n_row)
    upper = subtract(bem_entries, uppers[:-1], 0, half, (upper,))
    upper = finish(upper, bem_entries, uppers[-1], 0)
    second = gather_rows(upper, n_row)
    near, far = both_cores(join(first, (upper,)), n_row)
    pivots = [product(pivot_inverse, order, near, far, after=(upper,))]
    first = gather_rows(pivots[0], n_row)
    near, far = both_cores(join(second, (pivots[0],)), n_row)
    pivots.append(product(pivot_inverse, order, near, far, after=(pivots[0],)))
    second = gather_rows(pivots[1], n_row)
    near, far = both_cores(join(first, (pivots[1],)), n_row)
    below = subtract(bem_entries, lowers, 1, half, (pivots[1],))
    belows = [product(slab_below, order, near, far, lower, (below,))]
    near, far = both_cores(join(second, (belows[0],)), n_row)
    belows.append(product(slab_below, order, near, far, below))
    return jnp.stack([jnp.concatenate(parts, axis=1) for parts in (pivots, belows)])


def solution(mesh):
    placed = (
        P("row", "col"),
        P("col", None, None),
        P("col"),
        P("col"),
        P(None, "row"),
        P(None, "row", "col"),
        P("row", None),
        P("row", None),
    )
    return jax.shard_map(
        per_device, mesh=mesh, in_specs=placed, out_specs=P(None, "row", "col"), check_vma=False
    )
```

```python
import functools

import jax
import jax.numpy as jnp
from jax import lax
from jax.experimental import pallas as pl
from jax.experimental.pallas import tpu as pltpu
from jax.sharding import PartitionSpec as P

TILE = 128
STACK = 4
REPEATS = 32
VMEM_BYTES = 56 * 1024 * 1024


def largest_tile(total, most):
    best = total
    for size in range(16, most + 1, 16):
        if total % size == 0:
            best = size
    return best


def kernel_params():
    return pltpu.CompilerParams(vmem_limit_bytes=VMEM_BYTES)


def declared(flops=0):
    return pl.CostEstimate(flops=flops, bytes_accessed=1, transcendentals=0)


def whole_block(*shape):
    return pl.BlockSpec(shape, lambda *_: (0,) * len(shape))


def in_place():
    return pl.BlockSpec(memory_space=pl.ANY)


def dot32(left, right):
    return jnp.dot(left, right, preferred_element_type=jnp.float32)


def front_kernel(subs, flats, n_col, n_after, meta_ref, tiles_ref, front_ref, *refs):
    outs = refs[n_after : n_after + len(subs)]
    stack, held, acc, places, groups_of, state, tile_sems, sems = refs[n_after + len(subs) :]
    groups = n_col * len(subs)
    block, streams = held.shape[1], sems.shape[1]
    lines = block // streams
    step = pl.program_id(0)
    slot = lax.rem(step, 2)

    def front_copy(at, into, q):
        return pltpu.make_async_copy(
            front_ref.at[pl.ds(pl.multiple_of(at * block + q * lines, lines), lines), :],
            held.at[into, pl.ds(q * lines, lines), :],
            sems.at[into, q],
        )

    def tile_copy(t, item, place):
        return pltpu.make_async_copy(
            tiles_ref.at[t],
            stack.at[item, pl.ds(pl.multiple_of(place * TILE, TILE), TILE), :],
            tile_sems.at[t],
        )

    def chosen(t):
        return functools.reduce(jnp.logical_or, [meta_ref[2, t] == sub for sub in subs])

    def group_of(t):
        order = 0
        for p in range(1, len(subs)):
            order = jnp.where(meta_ref[2, t] == subs[p], p, order)
        return order * n_col + meta_ref[1, t]

    def clear(item, place):
        places[item, place] = 0
        stack[item, pl.ds(pl.multiple_of(place * TILE, TILE), TILE), :] = jnp.zeros(
            (TILE, TILE), stack.dtype
        )

    @pl.when(step == 0)
    def build():
        for q in range(streams):
            front_copy(0, 0, q).start()
        for g in range(groups):
            state[g] = 0
            state[groups + g] = 0
        state[2 * groups] = 0

        @pl.loop(0, tiles_ref.shape[0])
        def place_tile(t):
            @pl.when(chosen(t))
            def _():
                g = group_of(t)
                at = state[g]

                @pl.when(lax.rem(at, STACK) == 0)
                def _():
                    state[groups + g] = state[2 * groups]
                    groups_of[state[2 * groups]] = g
                    state[2 * groups] += 1

                item = state[groups + g]
                places[item, lax.rem(at, STACK)] = meta_ref[0, t]
                tile_copy(t, item, lax.rem(at, STACK)).start()
                state[g] = at + 1

        for g in range(groups):
            used = lax.rem(state[g], STACK)

            @pl.loop(used, jnp.where(used == 0, 0, STACK))
            def fill(place):
                clear(state[groups + g], place)

        items = state[2 * groups]

        @pl.loop(items, (items + STACK - 1) // STACK * STACK)
        def fill_item(item):
            groups_of[item] = 0
            for place in range(STACK):
                clear(item, place)

        @pl.loop(0, tiles_ref.shape[0])
        def wait_tile(t):
            @pl.when(chosen(t))
            def _():
                tile_copy(t, 0, 0).wait()

    @pl.when(step + 1 < pl.num_programs(0))
    def ahead():
        for q in range(streams):
            front_copy(step + 1, 1 - slot, q).start()

    for q in range(streams):
        front_copy(step, slot, q).wait()

    acc[...] = jnp.zeros_like(acc)

    @pl.loop(0, (state[2 * groups] + STACK - 1) // STACK)
    def add(s):
        for i in range(STACK):
            item = s * STACK + i
            lefts = [pl.multiple_of(places[item, j] * TILE, TILE) for j in range(STACK)]
            rows = [held[slot, :, pl.ds(left, TILE)] for left in lefts]
            acc[groups_of[item]] += dot32(jnp.concatenate(rows, axis=1), stack[item])

    for g in range(groups):
        out, dest = outs[g // n_col], g % n_col
        if flats[g // n_col]:
            out[:, dest * TILE : (dest + 1) * TILE] = acc[g].astype(out.dtype)
        else:
            out[dest] = acc[g].astype(out.dtype)


def front_products(front, tiles, meta, subs, flats, n_col, after=()):
    rows, depth = front.shape
    groups = n_col * len(subs)
    block = largest_tile(rows, 512)
    streams = 8 if block % 128 == 0 else 1
    count = tiles.shape[0]
    items = (-(-count // STACK) + groups + STACK) // STACK * STACK
    shapes, specs = [], []
    for flat in flats:
        if flat:
            shapes.append((rows, n_col * TILE))
            specs.append(pl.BlockSpec((block, n_col * TILE), lambda i, m: (i, 0)))
        else:
            shapes.append((n_col, rows, TILE))
            specs.append(pl.BlockSpec((n_col, block, TILE), lambda i, m: (0, i, 0)))
    return pl.pallas_call(
        functools.partial(front_kernel, subs, flats, n_col, len(after)),
        grid_spec=pltpu.PrefetchScalarGridSpec(
            num_scalar_prefetch=1,
            grid=(rows // block,),
            in_specs=[in_place()] * (2 + len(after)),
            out_specs=specs,
            scratch_shapes=[
                pltpu.VMEM((items, STACK * TILE, TILE), front.dtype),
                pltpu.VMEM((2, block, depth), front.dtype),
                pltpu.VMEM((groups, block, TILE), jnp.float32),
                pltpu.SMEM((items, STACK), jnp.int32),
                pltpu.SMEM((items,), jnp.int32),
                pltpu.SMEM((2 * groups + 1,), jnp.int32),
                pltpu.SemaphoreType.DMA((count,)),
                pltpu.SemaphoreType.DMA((2, streams)),
            ],
        ),
        out_shape=[jax.ShapeDtypeStruct(shape, front.dtype) for shape in shapes],
        compiler_params=kernel_params(),
        cost_estimate=declared(),
        name="front_products",
    )(meta, tiles, front, *after)


def one_hot(want, depth, kind):
    places = lax.broadcasted_iota(jnp.int32, (want.shape[0], depth), 1)
    return (places == want).astype(jnp.float32).astype(kind)


def pack_kernel(n_row, n_solved, index_ref, *refs):
    outs = refs[-2:]
    solved = jnp.concatenate([ref[...] for ref in refs[:n_solved]], axis=1)
    cap = outs[0].shape[0] * 2 // n_row
    for k in range(n_row):
        picks = one_hot(index_ref[k * cap : (k + 1) * cap, :], solved.shape[0], solved.dtype)
        at = k // 2 * cap
        outs[k % 2][at : at + cap, :] = dot32(picks, solved).astype(outs[0].dtype)


def pack_rows(index, solved, n_row, cap, after=(), share=0):
    depth = solved[0].shape[0]
    width = sum(part.shape[1] for part in solved)
    return pl.pallas_call(
        functools.partial(pack_kernel, n_row, len(solved)),
        in_specs=[whole_block(*index.shape)]
        + [whole_block(*part.shape) for part in solved]
        + [in_place()] * len(after),
        out_shape=[jax.ShapeDtypeStruct((n_row // 2 * cap, width), solved[0].dtype)] * 2,
        compiler_params=kernel_params(),
        cost_estimate=declared(share * n_row * cap * depth * width),
        name="pack_rows",
    )(index, *solved, *after)


def join_pieces(pieces, joined):
    at = 0
    for piece in pieces:
        joined[at : at + piece.shape[0], :] = piece[...]
        at += piece.shape[0]


def assemble_kernel(n_pieces, index_ref, bem_ref, *refs):
    outs, joined = refs[-3:-1], refs[-1]
    join_pieces(refs[:n_pieces], joined)
    count = outs[0].shape[0]
    step = largest_tile(count, 512)
    for half, out in enumerate(outs):
        for i in range(0, count, step):
            want = index_ref[half * count + i : half * count + i + step, :]
            taken = dot32(one_hot(want, joined.shape[0], joined.dtype), joined[...])
            entries = bem_ref[half, i : i + step, :].astype(jnp.float32)
            out[i : i + step, :] = (entries - taken).astype(out.dtype)


def assemble(index, bem, pieces, start, after=()):
    width = pieces[0].shape[1]
    routed = sum(piece.shape[0] for piece in pieces)
    count = bem.shape[1]
    place = start * TILE // width
    return pl.pallas_call(
        functools.partial(assemble_kernel, len(pieces)),
        grid=(1,),
        in_specs=[
            whole_block(*index.shape),
            pl.BlockSpec((2, count, width), lambda i: (0, 0, place)),
        ]
        + [whole_block(*piece.shape) for piece in pieces]
        + [in_place()] * len(after),
        out_specs=[whole_block(count, width)] * 2,
        out_shape=[jax.ShapeDtypeStruct((count, width), bem.dtype)] * 2,
        scratch_shapes=[pltpu.VMEM((routed, width), bem.dtype)],
        compiler_params=kernel_params(),
        cost_estimate=declared(4 * 2 * count * routed * width),
        name="assemble",
    )(index, bem, *pieces, *after)


def subtract_kernel(n_parts, bem_ref, *refs):
    out = refs[-1]
    for at, part in enumerate(refs[:n_parts]):
        columns = slice(at * TILE, (at + 1) * TILE)
        taken = part[...].astype(jnp.float32)
        out[:, columns] = (bem_ref[0, :, columns].astype(jnp.float32) - taken).astype(out.dtype)


def subtract(bem, parts, half, start, after=()):
    count, width = bem.shape[1], len(parts) * TILE
    place = start * TILE // width

    def rows_of(part):
        at = half if part.shape[0] > count else 0
        return pl.BlockSpec((count, TILE), lambda i: (at, 0))

    return pl.pallas_call(
        functools.partial(subtract_kernel, len(parts)),
        grid=(1,),
        in_specs=[pl.BlockSpec((1, count, width), lambda i: (half, 0, place))]
        + [rows_of(part) for part in parts]
        + [in_place()] * len(after),
        out_specs=whole_block(count, width),
        out_shape=jax.ShapeDtypeStruct((count, width), bem.dtype),
        compiler_params=kernel_params(),
        cost_estimate=declared(),
        name="subtract",
    )(bem, *parts, *after)


def finish_kernel(ready, ready_ref, bem_ref, schur_ref, *refs):
    out = refs[-1]
    out[:, :ready] = ready_ref[...]
    taken = schur_ref[...].astype(jnp.float32)
    out[:, ready:] = (bem_ref[0].astype(jnp.float32) - taken).astype(out.dtype)


def finish(ready, bem, schur, half, after=()):
    (count, width), last = ready.shape, schur.shape[1]
    place = bem.shape[2] // last - 1
    return pl.pallas_call(
        functools.partial(finish_kernel, width),
        grid=(1,),
        in_specs=[
            whole_block(count, width),
            pl.BlockSpec((1, count, last), lambda i: (half, 0, place)),
            whole_block(count, last),
        ]
        + [in_place()] * len(after),
        out_specs=whole_block(count, width + last),
        out_shape=jax.ShapeDtypeStruct((count, width + last), bem.dtype),
        compiler_params=kernel_params(),
        cost_estimate=declared(),
        name="finish",
    )(ready, bem, schur, *after)


def join_kernel(n_parts, *refs):
    join_pieces(refs[:n_parts], refs[-1])


def join(parts, after=()):
    depth, width = sum(part.shape[0] for part in parts), parts[0].shape[1]
    return pl.pallas_call(
        functools.partial(join_kernel, len(parts)),
        in_specs=[whole_block(*part.shape) for part in parts] + [in_place()] * len(after),
        out_shape=jax.ShapeDtypeStruct((depth, width), parts[0].dtype),
        compiler_params=kernel_params(),
        cost_estimate=declared(),
        name="join",
    )(*parts, *after)


def unpack_kernel(n_pieces, n_col, parts, index_ref, *refs):
    outs, joined = refs[-1 - parts : -1], refs[-1]
    join_pieces(refs[:n_pieces], joined)
    _, count, width = outs[0].shape
    step = largest_tile(count, 512)
    for p, out in enumerate(outs):
        for i in range(0, count, step):
            want = index_ref[p * count + i : p * count + i + step, :]
            taken = dot32(one_hot(want, joined.shape[0], joined.dtype), joined[...])
            for d in range(n_col):
                out[d, i : i + step, :] = taken[:, d * width : (d + 1) * width].astype(out.dtype)


def unpack(index, pieces, n_col, parts, after=(), share=0):
    wide = pieces[0].shape[1]
    routed = sum(piece.shape[0] for piece in pieces)
    count, width = index.shape[0] // parts, wide // n_col
    return pl.pallas_call(
        functools.partial(unpack_kernel, len(pieces), n_col, parts),
        in_specs=[whole_block(*index.shape)]
        + [whole_block(*piece.shape) for piece in pieces]
        + [in_place()] * len(after),
        out_shape=[jax.ShapeDtypeStruct((n_col, count, width), pieces[0].dtype)] * parts,
        scratch_shapes=[pltpu.VMEM((routed, wide), pieces[0].dtype)],
        compiler_params=kernel_params(),
        cost_estimate=declared(share * parts * count * routed * wide),
        name="unpack",
    )(index, *pieces, *after)


def product_kernel(streams, minus, order_ref, *refs):
    blocks, (near_ref, far_ref) = refs[:streams], refs[streams : streams + 2]
    out_ref, acc = refs[-2:]
    k = pl.program_id(0)
    steps = pl.num_programs(0)
    half = steps // 2
    deep = near_ref.shape[0] // half

    def term(rows_ref, at):
        matrix = jnp.concatenate([block[...] for block in blocks], axis=1)
        return dot32(matrix, rows_ref[pl.ds(pl.multiple_of(at * deep, deep), deep), :])

    @pl.when(k == 0)
    def _():
        acc[...] = term(near_ref, 0)

    @pl.when((k > 0) & (k < half))
    def _():
        acc[...] += term(near_ref, k)

    @pl.when(k >= half)
    def _():
        acc[...] += term(far_ref, k - half)

    @pl.when(k == steps - 1)
    def _():
        total = acc[...]
        if minus:
            total = refs[streams + 2][...].astype(jnp.float32) - total
        out_ref[...] = total.astype(out_ref.dtype)


def product(matrix, order, near, far, base=None, after=()):
    rows, depth = matrix.shape
    width = near.shape[1]
    n_row = order.shape[0]
    deep = depth // n_row
    streams = 4 if deep % (4 * TILE) == 0 else 1
    bases = [] if base is None else [base]

    def block_of(q):
        return pl.BlockSpec((rows, deep // streams), lambda k, order: (0, order[k] * streams + q))

    return pl.pallas_call(
        functools.partial(product_kernel, streams, bool(bases)),
        grid_spec=pltpu.PrefetchScalarGridSpec(
            num_scalar_prefetch=1,
            grid=(n_row,),
            in_specs=[block_of(q) for q in range(streams)]
            + [whole_block(*near.shape)] * 2
            + [whole_block(rows, width)] * len(bases)
            + [in_place()] * len(after),
            out_specs=whole_block(rows, width),
            scratch_shapes=[pltpu.VMEM((rows, width), jnp.float32)],
        ),
        out_shape=jax.ShapeDtypeStruct((rows, width), near.dtype),
        compiler_params=kernel_params(),
        cost_estimate=declared(6 * rows * depth * max(width, 256)),
        name="product",
    )(order, *[matrix] * streams, near, far, *bases, *after)


def exchange(value, distance, n, axis="row"):
    return lax.ppermute(value, axis, [(i, i ^ distance) for i in range(n)])


def route(packed, n_row):
    near, far = packed[0], exchange(packed[1], 1, n_row)
    cap = near.shape[0] * 2 // n_row
    sent = []
    for i in range(1, n_row // 2):
        both = [near[i * cap : (i + 1) * cap], far[i * cap : (i + 1) * cap]]
        sent.append(jnp.concatenate(both, axis=0))
    pieces = [exchange(both, 2 * i, n_row) for i, both in enumerate(sent, 1)]
    return [near[:cap], far[:cap]] + pieces, tuple(sent)


def gather_rows(block, n_row):
    return [block] + [exchange(block, k, n_row) for k in range(2, n_row, 2)]


def both_cores(near, n_row):
    return near, exchange(near, 1, n_row)


def route_tables(surface_map, rows, n_row, cap, slots):
    me = lax.axis_index("row")
    mine = surface_map.reshape(-1)
    shifts = jnp.arange(REPEATS, dtype=jnp.int32)[:, None]
    every = lax.all_gather(mine[None, :] + shifts, "row")[:, 0]
    partners = me ^ jnp.arange(n_row, dtype=jnp.int32)
    local = every[partners] - me * rows
    asked = (local >= 0) & (local < rows)
    rank = jnp.cumsum(asked.astype(jnp.int32), axis=1) - 1
    numbers = jnp.arange(slots, dtype=jnp.int32)
    hit = asked[:, None, :] & (rank[:, None, :] == numbers[None, :, None])
    wanted = jnp.sum(jnp.where(hit, local[:, None, :] + 1, 0), axis=2) - 1
    owner = mine // rows
    held = owner[None, :] == jnp.arange(n_row, dtype=jnp.int32)[:, None]
    place = jnp.cumsum(held.astype(jnp.int32), axis=1) - 1
    slot = jnp.sum(jnp.where(held, place, 0), axis=0)
    lands = (owner ^ me) * slots + slot
    return wanted.reshape(-1, 1), lands.reshape(-1, 1)


def per_device(
    front_inverse,
    coupling_tiles,
    tile_row,
    tile_col,
    surface_map,
    bem_entries,
    pivot_inverse,
    slab_below,
):
    n_row, n_col = lax.axis_size("row"), lax.axis_size("col")
    assert n_row > 1 and n_row & (n_row - 1) == 0
    rows, depth = front_inverse.shape
    count = bem_entries.shape[1]
    per_dest = bem_entries.shape[2] // TILE
    cap = rows // n_row
    slots = -(-cap // 16) * 16
    me = lax.axis_index("row")

    col_at = lax.axis_index("col")
    block_row = tile_row - col_at * (depth // TILE)
    dest, sub = tile_col // per_dest, tile_col % per_dest
    meta = jnp.stack([block_row, dest, sub])
    order = me ^ jnp.concatenate(
        [jnp.arange(0, n_row, 2, dtype=jnp.int32), jnp.arange(1, n_row, 2, dtype=jnp.int32)]
    )
    half = per_dest // 2
    assert per_dest == 2 * half

    def summed(parts):
        return lax.psum_scatter(parts, "col", scatter_dimension=0)

    parts = front_products(
        front_inverse, coupling_tiles, meta, tuple(range(half)), (False,) * half, n_col
    )
    solved = [summed(part) for part in parts]
    flats = front_products(
        front_inverse, coupling_tiles, meta, tuple(range(half, per_dest)), (True,) * half, n_col,
        (parts[0],),
    )
    wanted, lands = route_tables(surface_map, rows, n_row, cap, slots)
    routed, after = [], ()
    for flat in flats:
        packed = pack_rows(wanted, [flat], n_row, slots, after)
        pieces, after = route(packed, n_row)
        routed.append(pieces)
    after = (packed[0],)

    uppers, lowers = [], []
    for at, pieces in enumerate(routed):
        cuts = unpack(lands, pieces, n_col, 1 if at + 1 < half else 2, after, 0 if at else 12)
        uppers.append(summed(cuts[0]))
        lowers.append(cuts[1:])
        after = (cuts[0],)
        if at == 0:
            packed = pack_rows(wanted, solved, n_row, slots, after, 12)
            after = (packed[0],)
    lowers = [summed(low[0]) if low else both for low, both in zip(lowers, uppers)]

    upper, lower = assemble(lands, bem_entries, route(packed, n_row)[0], 0, after)
    first = gather_rows(upper, n_row)
    upper = subtract(bem_entries, uppers[:-1], 0, half, (upper,))
    upper = finish(upper, bem_entries, uppers[-1], 0)
    second = gather_rows(upper, n_row)
    near, far = both_cores(join(first, (upper,)), n_row)
    pivots = [product(pivot_inverse, order, near, far, after=(upper,))]
    first = gather_rows(pivots[0], n_row)
    near, far = both_cores(join(second, (pivots[0],)), n_row)
    pivots.append(product(pivot_inverse, order, near, far, after=(pivots[0],)))
    second = gather_rows(pivots[1], n_row)
    near, far = both_cores(join(first, (pivots[1],)), n_row)
    below = subtract(bem_entries, lowers, 1, half, (pivots[1],))
    belows = [product(slab_below, order, near, far, lower, (below,))]
    near, far = both_cores(join(second, (belows[0],)), n_row)
    belows.append(product(slab_below, order, near, far, below))
    return jnp.stack([jnp.concatenate(parts, axis=1) for parts in (pivots, belows)])


def solution(mesh):
    placed = (
        P("row", "col"),
        P("col", None, None),
        P("col"),
        P("col"),
        P(None, "row"),
        P(None, "row", "col"),
        P("row", None),
        P("row", None),
    )
    return jax.shard_map(
        per_device, mesh=mesh, in_specs=placed, out_specs=P(None, "row", "col"), check_vma=False
    )
```

```python
import functools

import jax
import jax.numpy as jnp
from jax import lax
from jax.experimental import pallas as pl
from jax.experimental.pallas import tpu as pltpu
from jax.sharding import PartitionSpec as P

TILE = 128
STACK = 4
REPEATS = 32
VMEM_BYTES = 56 * 1024 * 1024


def largest_tile(total, most):
    best = total
    for size in range(16, most + 1, 16):
        if total % size == 0:
            best = size
    return best


def kernel_params():
    return pltpu.CompilerParams(vmem_limit_bytes=VMEM_BYTES)


def declared(flops=0):
    return pl.CostEstimate(flops=flops, bytes_accessed=1, transcendentals=0)


def whole_block(*shape):
    return pl.BlockSpec(shape, lambda *_: (0,) * len(shape))


def in_place():
    return pl.BlockSpec(memory_space=pl.ANY)


def dot32(left, right):
    return jnp.dot(left, right, preferred_element_type=jnp.float32)


def front_kernel(subs, flats, n_col, n_after, meta_ref, tiles_ref, front_ref, *refs):
    outs = refs[n_after : n_after + len(subs)]
    stack, held, acc, places, groups_of, state, tile_sems, sems = refs[n_after + len(subs) :]
    groups = n_col * len(subs)
    block, streams = held.shape[1], sems.shape[1]
    lines = block // streams
    step = pl.program_id(0)
    slot = lax.rem(step, 2)

    def front_copy(at, into, q):
        return pltpu.make_async_copy(
            front_ref.at[pl.ds(pl.multiple_of(at * block + q * lines, lines), lines), :],
            held.at[into, pl.ds(q * lines, lines), :],
            sems.at[into, q],
        )

    def tile_copy(t, item, place):
        return pltpu.make_async_copy(
            tiles_ref.at[t],
            stack.at[item, pl.ds(pl.multiple_of(place * TILE, TILE), TILE), :],
            tile_sems.at[t],
        )

    def chosen(t):
        return functools.reduce(jnp.logical_or, [meta_ref[2, t] == sub for sub in subs])

    def group_of(t):
        order = 0
        for p in range(1, len(subs)):
            order = jnp.where(meta_ref[2, t] == subs[p], p, order)
        return order * n_col + meta_ref[1, t]

    def clear(item, place):
        places[item, place] = 0
        stack[item, pl.ds(pl.multiple_of(place * TILE, TILE), TILE), :] = jnp.zeros(
            (TILE, TILE), stack.dtype
        )

    @pl.when(step == 0)
    def build():
        for q in range(streams):
            front_copy(0, 0, q).start()
        for g in range(groups):
            state[g] = 0
            state[groups + g] = 0
        state[2 * groups] = 0

        @pl.loop(0, tiles_ref.shape[0])
        def place_tile(t):
            @pl.when(chosen(t))
            def _():
                g = group_of(t)
                at = state[g]

                @pl.when(lax.rem(at, STACK) == 0)
                def _():
                    state[groups + g] = state[2 * groups]
                    groups_of[state[2 * groups]] = g
                    state[2 * groups] += 1

                item = state[groups + g]
                places[item, lax.rem(at, STACK)] = meta_ref[0, t]
                tile_copy(t, item, lax.rem(at, STACK)).start()
                state[g] = at + 1

        for g in range(groups):
            used = lax.rem(state[g], STACK)

            @pl.loop(used, jnp.where(used == 0, 0, STACK))
            def fill(place):
                clear(state[groups + g], place)

        items = state[2 * groups]

        @pl.loop(items, (items + STACK - 1) // STACK * STACK)
        def fill_item(item):
            groups_of[item] = 0
            for place in range(STACK):
                clear(item, place)

        @pl.loop(0, tiles_ref.shape[0])
        def wait_tile(t):
            @pl.when(chosen(t))
            def _():
                tile_copy(t, 0, 0).wait()

    @pl.when(step + 1 < pl.num_programs(0))
    def ahead():
        for q in range(streams):
            front_copy(step + 1, 1 - slot, q).start()

    for q in range(streams):
        front_copy(step, slot, q).wait()

    acc[...] = jnp.zeros_like(acc)

    @pl.loop(0, (state[2 * groups] + STACK - 1) // STACK)
    def add(s):
        for i in range(STACK):
            item = s * STACK + i
            lefts = [pl.multiple_of(places[item, j] * TILE, TILE) for j in range(STACK)]
            rows = [held[slot, :, pl.ds(left, TILE)] for left in lefts]
            acc[groups_of[item]] += dot32(jnp.concatenate(rows, axis=1), stack[item])

    for g in range(groups):
        out, dest = outs[g // n_col], g % n_col
        if flats[g // n_col]:
            out[:, dest * TILE : (dest + 1) * TILE] = acc[g].astype(out.dtype)
        else:
            out[dest] = acc[g].astype(out.dtype)


def front_products(front, tiles, meta, subs, flats, n_col, after=()):
    rows, depth = front.shape
    groups = n_col * len(subs)
    block = largest_tile(rows, 1024)
    streams = 8 if block % 128 == 0 else 1
    count = tiles.shape[0]
    items = (-(-count // STACK) + groups + STACK) // STACK * STACK
    shapes, specs = [], []
    for flat in flats:
        if flat:
            shapes.append((rows, n_col * TILE))
            specs.append(pl.BlockSpec((block, n_col * TILE), lambda i, m: (i, 0)))
        else:
            shapes.append((n_col, rows, TILE))
            specs.append(pl.BlockSpec((n_col, block, TILE), lambda i, m: (0, i, 0)))
    return pl.pallas_call(
        functools.partial(front_kernel, subs, flats, n_col, len(after)),
        grid_spec=pltpu.PrefetchScalarGridSpec(
            num_scalar_prefetch=1,
            grid=(rows // block,),
            in_specs=[in_place()] * (2 + len(after)),
            out_specs=specs,
            scratch_shapes=[
                pltpu.VMEM((items, STACK * TILE, TILE), front.dtype),
                pltpu.VMEM((2, block, depth), front.dtype),
                pltpu.VMEM((groups, block, TILE), jnp.float32),
                pltpu.SMEM((items, STACK), jnp.int32),
                pltpu.SMEM((items,), jnp.int32),
                pltpu.SMEM((2 * groups + 1,), jnp.int32),
                pltpu.SemaphoreType.DMA((count,)),
                pltpu.SemaphoreType.DMA((2, streams)),
            ],
        ),
        out_shape=[jax.ShapeDtypeStruct(shape, front.dtype) for shape in shapes],
        compiler_params=kernel_params(),
        cost_estimate=declared(),
        name="front_products",
    )(meta, tiles, front, *after)


def one_hot(want, depth, kind):
    places = lax.broadcasted_iota(jnp.int32, (want.shape[0], depth), 1)
    return (places == want).astype(jnp.float32).astype(kind)


def pack_kernel(n_row, n_solved, index_ref, *refs):
    outs = refs[-2:]
    solved = jnp.concatenate([ref[...] for ref in refs[:n_solved]], axis=1)
    cap = outs[0].shape[0] * 2 // n_row
    for k in range(n_row):
        picks = one_hot(index_ref[k * cap : (k + 1) * cap, :], solved.shape[0], solved.dtype)
        at = k // 2 * cap
        outs[k % 2][at : at + cap, :] = dot32(picks, solved).astype(outs[0].dtype)


def pack_rows(index, solved, n_row, cap, after=(), share=0):
    depth = solved[0].shape[0]
    width = sum(part.shape[1] for part in solved)
    return pl.pallas_call(
        functools.partial(pack_kernel, n_row, len(solved)),
        in_specs=[whole_block(*index.shape)]
        + [whole_block(*part.shape) for part in solved]
        + [in_place()] * len(after),
        out_shape=[jax.ShapeDtypeStruct((n_row // 2 * cap, width), solved[0].dtype)] * 2,
        compiler_params=kernel_params(),
        cost_estimate=declared(share * n_row * cap * depth * width),
        name="pack_rows",
    )(index, *solved, *after)


def join_pieces(pieces, joined):
    at = 0
    for piece in pieces:
        joined[at : at + piece.shape[0], :] = piece[...]
        at += piece.shape[0]


def assemble_kernel(n_pieces, index_ref, bem_ref, *refs):
    outs, joined = refs[-3:-1], refs[-1]
    join_pieces(refs[:n_pieces], joined)
    count = outs[0].shape[0]
    step = largest_tile(count, 512)
    for half, out in enumerate(outs):
        for i in range(0, count, step):
            want = index_ref[half * count + i : half * count + i + step, :]
            taken = dot32(one_hot(want, joined.shape[0], joined.dtype), joined[...])
            entries = bem_ref[half, i : i + step, :].astype(jnp.float32)
            out[i : i + step, :] = (entries - taken).astype(out.dtype)


def assemble(index, bem, pieces, start, after=()):
    width = pieces[0].shape[1]
    routed = sum(piece.shape[0] for piece in pieces)
    count = bem.shape[1]
    place = start * TILE // width
    return pl.pallas_call(
        functools.partial(assemble_kernel, len(pieces)),
        grid=(1,),
        in_specs=[
            whole_block(*index.shape),
            pl.BlockSpec((2, count, width), lambda i: (0, 0, place)),
        ]
        + [whole_block(*piece.shape) for piece in pieces]
        + [in_place()] * len(after),
        out_specs=[whole_block(count, width)] * 2,
        out_shape=[jax.ShapeDtypeStruct((count, width), bem.dtype)] * 2,
        scratch_shapes=[pltpu.VMEM((routed, width), bem.dtype)],
        compiler_params=kernel_params(),
        cost_estimate=declared(4 * 2 * count * routed * width),
        name="assemble",
    )(index, bem, *pieces, *after)


def subtract_kernel(n_parts, bem_ref, *refs):
    out = refs[-1]
    for at, part in enumerate(refs[:n_parts]):
        columns = slice(at * TILE, (at + 1) * TILE)
        taken = part[...].astype(jnp.float32)
        out[:, columns] = (bem_ref[0, :, columns].astype(jnp.float32) - taken).astype(out.dtype)


def subtract(bem, parts, half, start, after=()):
    count, width = bem.shape[1], len(parts) * TILE
    place = start * TILE // width

    def rows_of(part):
        at = half if part.shape[0] > count else 0
        return pl.BlockSpec((count, TILE), lambda i: (at, 0))

    return pl.pallas_call(
        functools.partial(subtract_kernel, len(parts)),
        grid=(1,),
        in_specs=[pl.BlockSpec((1, count, width), lambda i: (half, 0, place))]
        + [rows_of(part) for part in parts]
        + [in_place()] * len(after),
        out_specs=whole_block(count, width),
        out_shape=jax.ShapeDtypeStruct((count, width), bem.dtype),
        compiler_params=kernel_params(),
        cost_estimate=declared(),
        name="subtract",
    )(bem, *parts, *after)


def finish_kernel(ready, ready_ref, bem_ref, schur_ref, *refs):
    out = refs[-1]
    out[:, :ready] = ready_ref[...]
    taken = schur_ref[...].astype(jnp.float32)
    out[:, ready:] = (bem_ref[0].astype(jnp.float32) - taken).astype(out.dtype)


def finish(ready, bem, schur, half, after=()):
    (count, width), last = ready.shape, schur.shape[1]
    place = bem.shape[2] // last - 1
    return pl.pallas_call(
        functools.partial(finish_kernel, width),
        grid=(1,),
        in_specs=[
            whole_block(count, width),
            pl.BlockSpec((1, count, last), lambda i: (half, 0, place)),
            whole_block(count, last),
        ]
        + [in_place()] * len(after),
        out_specs=whole_block(count, width + last),
        out_shape=jax.ShapeDtypeStruct((count, width + last), bem.dtype),
        compiler_params=kernel_params(),
        cost_estimate=declared(),
        name="finish",
    )(ready, bem, schur, *after)


def join_kernel(n_parts, *refs):
    join_pieces(refs[:n_parts], refs[-1])


def join(parts, after=()):
    depth, width = sum(part.shape[0] for part in parts), parts[0].shape[1]
    return pl.pallas_call(
        functools.partial(join_kernel, len(parts)),
        in_specs=[whole_block(*part.shape) for part in parts] + [in_place()] * len(after),
        out_shape=jax.ShapeDtypeStruct((depth, width), parts[0].dtype),
        compiler_params=kernel_params(),
        cost_estimate=declared(),
        name="join",
    )(*parts, *after)


def unpack_kernel(n_pieces, n_col, parts, index_ref, *refs):
    outs, joined = refs[-1 - parts : -1], refs[-1]
    join_pieces(refs[:n_pieces], joined)
    _, count, width = outs[0].shape
    step = largest_tile(count, 512)
    for p, out in enumerate(outs):
        for i in range(0, count, step):
            want = index_ref[p * count + i : p * count + i + step, :]
            taken = dot32(one_hot(want, joined.shape[0], joined.dtype), joined[...])
            for d in range(n_col):
                out[d, i : i + step, :] = taken[:, d * width : (d + 1) * width].astype(out.dtype)


def unpack(index, pieces, n_col, parts, after=(), share=0):
    wide = pieces[0].shape[1]
    routed = sum(piece.shape[0] for piece in pieces)
    count, width = index.shape[0] // parts, wide // n_col
    return pl.pallas_call(
        functools.partial(unpack_kernel, len(pieces), n_col, parts),
        in_specs=[whole_block(*index.shape)]
        + [whole_block(*piece.shape) for piece in pieces]
        + [in_place()] * len(after),
        out_shape=[jax.ShapeDtypeStruct((n_col, count, width), pieces[0].dtype)] * parts,
        scratch_shapes=[pltpu.VMEM((routed, wide), pieces[0].dtype)],
        compiler_params=kernel_params(),
        cost_estimate=declared(share * parts * count * routed * wide),
        name="unpack",
    )(index, *pieces, *after)


def product_kernel(streams, minus, order_ref, *refs):
    blocks, (near_ref, far_ref) = refs[:streams], refs[streams : streams + 2]
    out_ref, acc = refs[-2:]
    k = pl.program_id(0)
    steps = pl.num_programs(0)
    half = steps // 2
    deep = near_ref.shape[0] // half

    def term(rows_ref, at):
        matrix = jnp.concatenate([block[...] for block in blocks], axis=1)
        return dot32(matrix, rows_ref[pl.ds(pl.multiple_of(at * deep, deep), deep), :])

    @pl.when(k == 0)
    def _():
        acc[...] = term(near_ref, 0)

    @pl.when((k > 0) & (k < half))
    def _():
        acc[...] += term(near_ref, k)

    @pl.when(k >= half)
    def _():
        acc[...] += term(far_ref, k - half)

    @pl.when(k == steps - 1)
    def _():
        total = acc[...]
        if minus:
            total = refs[streams + 2][...].astype(jnp.float32) - total
        out_ref[...] = total.astype(out_ref.dtype)


def product(matrix, order, near, far, base=None, after=()):
    rows, depth = matrix.shape
    width = near.shape[1]
    n_row = order.shape[0]
    deep = depth // n_row
    streams = 4 if deep % (4 * TILE) == 0 else 1
    bases = [] if base is None else [base]

    def block_of(q):
        return pl.BlockSpec((rows, deep // streams), lambda k, order: (0, order[k] * streams + q))

    return pl.pallas_call(
        functools.partial(product_kernel, streams, bool(bases)),
        grid_spec=pltpu.PrefetchScalarGridSpec(
            num_scalar_prefetch=1,
            grid=(n_row,),
            in_specs=[block_of(q) for q in range(streams)]
            + [whole_block(*near.shape)] * 2
            + [whole_block(rows, width)] * len(bases)
            + [in_place()] * len(after),
            out_specs=whole_block(rows, width),
            scratch_shapes=[pltpu.VMEM((rows, width), jnp.float32)],
        ),
        out_shape=jax.ShapeDtypeStruct((rows, width), near.dtype),
        compiler_params=kernel_params(),
        cost_estimate=declared(6 * rows * depth * max(width, 256)),
        name="product",
    )(order, *[matrix] * streams, near, far, *bases, *after)


def exchange(value, distance, n, axis="row"):
    return lax.ppermute(value, axis, [(i, i ^ distance) for i in range(n)])


def route(packed, n_row):
    near, far = packed[0], exchange(packed[1], 1, n_row)
    cap = near.shape[0] * 2 // n_row
    sent = []
    for i in range(1, n_row // 2):
        both = [near[i * cap : (i + 1) * cap], far[i * cap : (i + 1) * cap]]
        sent.append(jnp.concatenate(both, axis=0))
    pieces = [exchange(both, 2 * i, n_row) for i, both in enumerate(sent, 1)]
    return [near[:cap], far[:cap]] + pieces, tuple(sent)


def gather_rows(block, n_row):
    return [block] + [exchange(block, k, n_row) for k in range(2, n_row, 2)]


def both_cores(near, n_row):
    return near, exchange(near, 1, n_row)


def route_tables(surface_map, rows, n_row, cap, slots):
    me = lax.axis_index("row")
    mine = surface_map.reshape(-1)
    shifts = jnp.arange(REPEATS, dtype=jnp.int32)[:, None]
    every = lax.all_gather(mine[None, :] + shifts, "row")[:, 0]
    partners = me ^ jnp.arange(n_row, dtype=jnp.int32)
    local = every[partners] - me * rows
    asked = (local >= 0) & (local < rows)
    rank = jnp.cumsum(asked.astype(jnp.int32), axis=1) - 1
    numbers = jnp.arange(slots, dtype=jnp.int32)
    hit = asked[:, None, :] & (rank[:, None, :] == numbers[None, :, None])
    wanted = jnp.sum(jnp.where(hit, local[:, None, :] + 1, 0), axis=2) - 1
    owner = mine // rows
    held = owner[None, :] == jnp.arange(n_row, dtype=jnp.int32)[:, None]
    place = jnp.cumsum(held.astype(jnp.int32), axis=1) - 1
    slot = jnp.sum(jnp.where(held, place, 0), axis=0)
    lands = (owner ^ me) * slots + slot
    return wanted.reshape(-1, 1), lands.reshape(-1, 1)


def per_device(
    front_inverse,
    coupling_tiles,
    tile_row,
    tile_col,
    surface_map,
    bem_entries,
    pivot_inverse,
    slab_below,
):
    n_row, n_col = lax.axis_size("row"), lax.axis_size("col")
    assert n_row > 1 and n_row & (n_row - 1) == 0
    rows, depth = front_inverse.shape
    count = bem_entries.shape[1]
    per_dest = bem_entries.shape[2] // TILE
    cap = rows // n_row
    slots = -(-cap // 16) * 16
    me = lax.axis_index("row")

    col_at = lax.axis_index("col")
    block_row = tile_row - col_at * (depth // TILE)
    dest, sub = tile_col // per_dest, tile_col % per_dest
    meta = jnp.stack([block_row, dest, sub])
    order = me ^ jnp.concatenate(
        [jnp.arange(0, n_row, 2, dtype=jnp.int32), jnp.arange(1, n_row, 2, dtype=jnp.int32)]
    )
    half = per_dest // 2
    assert per_dest == 2 * half

    def summed(parts):
        return lax.psum_scatter(parts, "col", scatter_dimension=0)

    parts = front_products(
        front_inverse, coupling_tiles, meta, tuple(range(half)), (False,) * half, n_col
    )
    solved = [summed(part) for part in parts]
    flats = front_products(
        front_inverse, coupling_tiles, meta, tuple(range(half, per_dest)), (True,) * half, n_col,
        (parts[0],),
    )
    wanted, lands = route_tables(surface_map, rows, n_row, cap, slots)
    routed, after = [], ()
    for flat in flats:
        packed = pack_rows(wanted, [flat], n_row, slots, after)
        pieces, after = route(packed, n_row)
        routed.append(pieces)
    after = (packed[0],)

    uppers, lowers = [], []
    for at, pieces in enumerate(routed):
        cuts = unpack(lands, pieces, n_col, 1 if at + 1 < half else 2, after, 0 if at else 12)
        uppers.append(summed(cuts[0]))
        lowers.append(cuts[1:])
        after = (cuts[0],)
        if at == 0:
            packed = pack_rows(wanted, solved, n_row, slots, after, 12)
            after = (packed[0],)
    lowers = [summed(low[0]) if low else both for low, both in zip(lowers, uppers)]

    upper, lower = assemble(lands, bem_entries, route(packed, n_row)[0], 0, after)
    first = gather_rows(upper, n_row)
    upper = subtract(bem_entries, uppers[:-1], 0, half, (upper,))
    upper = finish(upper, bem_entries, uppers[-1], 0)
    second = gather_rows(upper, n_row)
    near, far = both_cores(join(first, (upper,)), n_row)
    pivots = [product(pivot_inverse, order, near, far, after=(upper,))]
    first = gather_rows(pivots[0], n_row)
    near, far = both_cores(join(second, (pivots[0],)), n_row)
    pivots.append(product(pivot_inverse, order, near, far, after=(pivots[0],)))
    second = gather_rows(pivots[1], n_row)
    near, far = both_cores(join(first, (pivots[1],)), n_row)
    below = subtract(bem_entries, lowers, 1, half, (pivots[1],))
    belows = [product(slab_below, order, near, far, lower, (below,))]
    near, far = both_cores(join(second, (belows[0],)), n_row)
    belows.append(product(slab_below, order, near, far, below))
    return jnp.stack([jnp.concatenate(parts, axis=1) for parts in (pivots, belows)])


def solution(mesh):
    placed = (
        P("row", "col"),
        P("col", None, None),
        P("col"),
        P("col"),
        P(None, "row"),
        P(None, "row", "col"),
        P("row", None),
        P("row", None),
    )
    return jax.shard_map(
        per_device, mesh=mesh, in_specs=placed, out_specs=P(None, "row", "col"), check_vma=False
    )
```
